512 devices in a mesh: section: 8 (over y_hi, core), dp: 64 (over y_lo, x, z).
Axes of the slice: x: 4, y: 8 (y_hi: 4, y_lo: 2; y = y_hi * 2 + y_lo), z: 8, core: 2. Of those that a mesh axis runs over, the one named last changes fastest.
Arguments:
- activations: bfloat16 [8, 16384, 2048], P('section', 'dp'), may hold values from -18 to 18
- norm_gain: bfloat16 [8, 2048], P('section'), may hold values from 0.099609375 to 1.8984375
- query_weight: bfloat16 [8, 2048, 2048], P('section', 'dp'), may hold values from -0.125 to 0.125
- keyval_weight: bfloat16 [8, 2048, 1024], P('section', 'dp'), may hold values from -0.25 to 0.25
- prefix_cache: bfloat16 [8, 32768, 1024], P('section', 'dp'), may hold values from -256 to 256
- random_blocks: int32 [128, 3], P('dp'), may hold values from 0 to 255, as said below
Outputs:
- section_output: bfloat16 [8, 16384, 2048], P('section', 'dp')
The draws below stay inside these ranges and needn't reach their ends.
Inputs may be any that keep to these rules, and one draw needn't show every extreme that they name: `random_blocks`: for each query block q, 3 different cache blocks, all from (q // 2) * 4 to (q // 2 + 1) * 4 - 1.
All inputs are finite; a program needn't handle non-finite values.
Results may differ from the reference program's by a relative error of at most 0.0055.
The reference program's roundings to bfloat16 on the way (of `normed`, `queries`, `keyvals`, `joined` and `probs`) count: a program that leaves them out, or rounds other values in their place, can miss the bound.
Values may be sent and summed in bfloat16 or wider, within the bound.
A program may use at most 64 MiB of HBM per device.

```python
import math
import jax
import jax.numpy as jnp
from jax import lax

D = 2048
H = 16
KVH = 4
HD = 128
BLK = 128
G = 2
R = 3
QB_DEV = 2
CB_DEV = 4
LAYERS = 8
QD = 2048
KVD = 512
TOKENS = 16384
QBLOCKS = 128
CACHE = 32768


def draw_activations(key, part):
    key = jax.random.fold_in(key, 11)
    first, second, third = jax.random.split(key, 3)
    base = jnp.clip(jax.random.normal(first, (LAYERS, TOKENS, D), jnp.float32), -6.0, 6.0)
    rows = jnp.exp(jax.random.uniform(second, (LAYERS, TOKENS, 1), jnp.float32, math.log(0.1), 0.0))
    columns = jnp.exp(jax.random.uniform(third, (1, 1, D), jnp.float32, math.log(0.3), math.log(3.0)))
    return (base * rows * columns).astype(jnp.bfloat16)


def draw_prefix_cache(key, part):
    key = jax.random.fold_in(key, 23)
    first = jax.random.fold_in(key, 0)
    base = 2.0 * jnp.clip(jax.random.normal(first, (LAYERS, CACHE, 2 * KVD), jnp.float32), -6.0, 6.0)
    return jnp.clip(base, -256.0, 256.0).astype(jnp.bfloat16)


def draw_random_blocks(key, part):
    key = jax.random.fold_in(key, 37)
    shifted = jax.random.randint(key, (QBLOCKS,), 0, CB_DEV, jnp.int32)
    shifted = shifted.at[0].set(0).at[QBLOCKS - 1].set(CB_DEV - R)
    stripes = jnp.arange(QBLOCKS, dtype=jnp.int32) // QB_DEV * CB_DEV
    offsets = (shifted[:, None] + jnp.arange(R, dtype=jnp.int32)[None, :]) % CB_DEV
    return (stripes[:, None] + offsets).astype(jnp.int32)


def steps_of(key, shape, pieces, smallest, top_value):
    level, own = 1.0, jax.random.fold_in(key, 6)
    for axis_at, parts in pieces:
        heights = jnp.exp(jax.random.uniform(jax.random.fold_in(own, axis_at), (parts,), jnp.float32, smallest / len(pieces), top_value / len(pieces)))
        level = level * jnp.repeat(heights, shape[axis_at] // parts).reshape([-1 if axis == axis_at else 1 for axis in range(len(shape))])
    return level


def gaussian(stream_key, dims, deviation, most, cuts=(), held_as=jnp.bfloat16):
    level = steps_of(stream_key, dims, cuts, -0.22, 0.18) if cuts else 1.0
    drawn = jax.random.normal(stream_key, dims, jnp.float32) * deviation * level
    return jnp.minimum(jnp.maximum(drawn, -most), most).astype(held_as)


def setup_inputs(seed: int = 0) -> dict:
    arg_keys = jax.random.split(jax.random.key(seed), 7)
    activations = draw_activations(jax.random.fold_in(arg_keys[6], 71), 0)
    norm_gain = jnp.clip(1.0 + 0.18 * jax.random.normal(arg_keys[1], (LAYERS, D), jnp.float32), 0.099609375, 1.8984375).astype(jnp.bfloat16)
    query_weight = gaussian(arg_keys[2], (LAYERS, D, QD), D ** -0.5, 0.125, ((0, 8), (1, 64)))
    keyval_weight = gaussian(arg_keys[3], (LAYERS, D, 2 * KVD), (D // 4) ** -0.5, 0.25, ((0, 8), (1, 64)))
    prefix_cache = draw_prefix_cache(jax.random.fold_in(arg_keys[6], 71), 0)
    random_blocks = draw_random_blocks(jax.random.fold_in(arg_keys[6], 71), 0)
    return dict(activations=activations, norm_gain=norm_gain, query_weight=query_weight, keyval_weight=keyval_weight, prefix_cache=prefix_cache, random_blocks=random_blocks)


epsilon = 1e-05

def normalize(residual, gain):
    widened = residual.astype(jnp.float32)
    spread = lax.optimization_barrier(jnp.mean(widened * widened, axis=-1, keepdims=True))
    return (widened * lax.rsqrt(spread + epsilon) * gain.astype(jnp.float32)).astype(jnp.bfloat16)

def visible(prior_valid):
    key_column = jnp.arange((G + R + 2) * BLK)[None, :]
    query_row = jnp.arange(BLK)[:, None]
    prior_start = (G + R) * BLK
    own_start = prior_start + BLK
    leading = key_column < prior_start
    prior_rows = (key_column >= prior_start) & (key_column < own_start) & prior_valid
    own_rows = (key_column >= own_start) & (key_column - own_start <= query_row)
    return leading | prior_rows | own_rows

def probabilities(scores, allowed):
    masked = jnp.where(allowed, scores, -jnp.inf)
    highest = lax.optimization_barrier(jnp.max(masked, axis=-1, keepdims=True))
    raised = jnp.exp(masked - highest)
    return (raised / lax.optimization_barrier(jnp.sum(raised, axis=-1, keepdims=True))).astype(jnp.bfloat16)

def layer(residual, gain, query_weight, keyval_weight, cache_rows, random_blocks):
    normed = normalize(residual, gain)
    queries = jnp.dot(normed, query_weight, preferred_element_type=jnp.float32).astype(jnp.bfloat16)
    keyvals = jnp.dot(normed, keyval_weight, preferred_element_type=jnp.float32).astype(jnp.bfloat16)
    groups = H // KVH
    width = KVH * HD
    query_blocks = queries.reshape(QBLOCKS, BLK, KVH, groups, HD)
    own_blocks = keyvals.reshape(QBLOCKS, BLK, 2 * width)
    prior_blocks = jnp.concatenate([jnp.zeros_like(own_blocks[:1]), own_blocks[:-1]], axis=0)
    cache_blocks = cache_rows.reshape(CACHE // BLK, BLK, 2 * width)
    global_rows = cache_blocks[:G].reshape(G * BLK, 2 * width)

    def one_block(packed):
        block_queries, prior_rows, own_rows, chosen, number = packed
        picked = jnp.take(cache_blocks, chosen.astype(jnp.int32), axis=0).reshape(R * BLK, 2 * width)
        joined = jnp.concatenate([global_rows, picked, prior_rows, own_rows], axis=0)
        key_rows = joined[:, :width].reshape(-1, KVH, HD).astype(jnp.float32)
        value_rows = joined[:, width:].reshape(-1, KVH, HD).astype(jnp.float32)
        scores = jnp.einsum('tkgd,skd->kgts', block_queries.astype(jnp.float32), key_rows) / math.sqrt(HD)
        probs = probabilities(scores, visible(number > 0))
        heads = jnp.einsum('kgts,skd->tkgd', probs.astype(jnp.float32), value_rows)
        return heads.reshape(BLK, H * HD)
    numbers = jnp.arange(QBLOCKS, dtype=jnp.int32)
    heads = lax.map(one_block, (query_blocks, prior_blocks, own_blocks, random_blocks, numbers))
    return residual.astype(jnp.float32) + heads.reshape(TOKENS, H * HD)

def reference(activations, norm_gain, query_weight, keyval_weight, prefix_cache, random_blocks):
    results = [layer(activations[layer_index], norm_gain[layer_index], query_weight[layer_index], keyval_weight[layer_index], prefix_cache[layer_index], random_blocks) for layer_index in range(LAYERS)]
    ordered = [results[(layer_index - 1) % LAYERS] for layer_index in range(LAYERS)]
    return jnp.stack(ordered).astype(jnp.bfloat16)
```

```python
import math

import jax
import jax.numpy as jnp
from jax import lax
from jax.experimental import pallas as pl
from jax.experimental.pallas import tpu as pltpu
from jax.sharding import PartitionSpec as P

KVH = 4
HD = 128
D = 2048
KVD = 512
TOK = 256
NX, NZ = 4, 8
ROWS = 32
EPS = 1e-05
MESH = pl.DeviceIdType.MESH
F32, BF16 = jnp.float32, jnp.bfloat16
SCALE = math.log2(math.e) / math.sqrt(HD)

PHASES = ((0, 512, 1024), (1024, 1280, 1536), (1536, 1792, 2048), (2048, 2304, 2560), (2560, 2816, 3072))
NP = len(PHASES)
NIN = 8


def kernel(
    act, gain, qw, kvw, cache, rb, out,
    W, G, res, nb, cbuf, kv, qb, ob, gown, gbuf, bown, bbuf,
    in_s, in_r, gs_s, gs_r, gx_s, gx_r, gz_s, gz_r, p1_s, p1_r, p2_s, p2_r, sib_s, sib_r, gsib_s, gsib_r,
    halo_s, halo_r, out_s, out_r,
):
    s, d = lax.axis_index("section"), lax.axis_index("dp")
    yh, c = lax.div(s, 2), lax.rem(s, 2)
    yl, xz = lax.div(d, 32), lax.rem(d, 32)
    x, z = lax.div(xz, NZ), lax.rem(xz, NZ)
    base = 32 * yl
    share, layer = 32 * c + xz, 2 * yh + yl
    swapped = c != yl

    def xat(k):
        return lax.rem(x + k + NX, NX)

    def zat(k):
        return lax.rem(z + k + NZ, NZ)

    def xdev(k):
        return (s, base + NZ * xat(k) + z)

    def zdev(k):
        return (s, base + NZ * x + zat(k))

    def worker(layer_, share_):
        return (2 * lax.div(layer_, 2) + lax.div(share_, 32), 32 * lax.rem(layer_, 2) + lax.rem(share_, 32))

    sibling = (2 * yh + 1 - c, d)
    partner = (2 * yh + 1 - c, 32 * (1 - yl) + xz)
    target = (lax.rem(layer + 1, 8), share)
    origin = worker(lax.rem(s + 7, 8), d)
    is_source = d == 0

    bar = pltpu.get_barrier_semaphore()

    def greet(dev):
        pl.semaphore_signal(bar, inc=1, device_id=dev, device_id_type=MESH)

    for dev in (xdev(1), xdev(-1), xdev(2), zdev(1), zdev(-1), sibling, origin):
        greet(dev)
    pl.when(swapped)(lambda: greet(partner))
    pl.when(share > 0)(lambda: greet(worker(layer, share - 1)))
    scattered = (x == 0) & jnp.logical_not((d == 0) & (c == 0))
    pl.when(scattered)(lambda: greet((layer, 0)))

    gown[...] = jnp.broadcast_to(gain[...].astype(F32), (8, D))
    blocks = lax.broadcasted_iota(jnp.int32, (8, 512), 1) // 128 + 4 * d
    row = lax.broadcasted_iota(jnp.int32, (8, 512), 0)
    picked = [
        (blocks == rb[b, 0]) | (blocks == rb[b, 1]) | (blocks == rb[b, 2]) for b in range(2)
    ]
    zero, never = jnp.zeros((8, 512), F32), jnp.full((8, 512), -jnp.inf, F32)
    bown[...] = jnp.where(row == 0, jnp.where(picked[0], zero, never), jnp.where(picked[1], zero, never))

    extra = jnp.where(is_source, 15 + c, 0)
    pl.semaphore_wait(bar, 7 + swapped.astype(jnp.int32) + (share < 63).astype(jnp.int32) + extra)

    sends = []

    def push(src, dst, send, recv, dev):
        copy = pltpu.make_async_remote_copy(src, dst, send, recv, device_id=dev, device_id_type=MESH)
        copy.start()
        sends.append(copy)

    def arrived(ref, sem):
        pltpu.make_async_copy(ref, ref, sem).wait()

    def entries(slot):
        return (
            (kvw.at[0], W.at[slot, x, z, :, 0:1024]),
            (qw.at[0], W.at[slot, x, z, :, 1024:3072]),
            (gown, gbuf),
            (act.at[0], res),
            (bown, bbuf),
            (cache.at[0, :, 0:256], cbuf.at[:, 0:256]),
            (cache.at[0, :, 512:768], cbuf.at[:, 512:768]),
            (cache.at[0, :, 256:512], cbuf.at[:, 256:512]),
            (cache.at[0, :, 768:1024], cbuf.at[:, 768:1024]),
        )

    def bring(first, last):
        def own():
            for k in range(first, last):
                src, dst = entries(yl)[k]
                pltpu.make_async_copy(src, dst, in_r.at[k]).start()

        def trade():
            for k in range(first, last):
                src, dst = entries(yl)[k]
                pltpu.make_async_remote_copy(
                    src, dst, in_s.at[k], in_r.at[k], device_id=partner, device_id_type=MESH
                ).start()

        pl.when(jnp.logical_not(swapped))(own)
        pl.when(swapped)(trade)

    def brought(k):
        arrived(entries(c)[k][1], in_r.at[k])

    def scatter_copy(ct, zt):
        return pltpu.make_async_remote_copy(
            cache.at[0, ROWS * zt : ROWS * zt + ROWS, 512 * ct : 512 * ct + 512], G.at[ct, zt],
            gs_s.at[8 * ct + zt], gs_r.at[0],
            device_id=(2 * yh + ct, 32 * c + zt), device_id_type=MESH,
        )

    def scatter(act_on):
        for ct in range(2):
            for zt in range(8):
                if (ct, zt) == (0, 0):
                    pl.when(c == 1)(lambda: act_on(scatter_copy(0, 0)))
                else:
                    act_on(scatter_copy(ct, zt))

    def globals_round():
        pl.when(x == 0)(lambda: arrived(G.at[c, z], gs_r.at[0]))

        def spread():
            for k in range(1, NX):
                pltpu.make_async_remote_copy(
                    G.at[c, z], G.at[c, z], gx_s.at[k - 1], gx_r.at[0], device_id=xdev(k), device_id_type=MESH
                ).start()

        pl.when(x == 0)(spread)
        yield
        pl.when(x != 0)(lambda: arrived(G.at[c, z], gx_r.at[0]))
        for k in range(4):
            a, b = (slice(0, 16), slice(16, 32)) if k == 3 else (slice(0, 32),) * 2
            push(G.at[c, zat(-k), a], G.at[c, zat(-k), a], gz_s.at[2 * k], gz_r.at[2 * k], zdev(1))
            push(G.at[c, zat(k), b], G.at[c, zat(k), b], gz_s.at[2 * k + 1], gz_r.at[2 * k + 1], zdev(-1))
            yield
            arrived(G.at[c, zat(-k - 1), a], gz_r.at[2 * k])
            arrived(G.at[c, zat(k + 1), b], gz_r.at[2 * k + 1])
        push(G.at[c], G.at[c], gsib_s.at[0], gsib_r.at[0], sibling)

    def x_then_z(p):
        cols = slice(PHASES[p][0], PHASES[p][1])
        mine = W.at[c, x, z, :, cols]
        for i, k in enumerate((1, -1, 2)):
            push(mine, mine, p1_s.at[p, i], p1_r.at[p, i], xdev(k))
        yield
        for i, k in enumerate((-1, 1, 2)):
            arrived(W.at[c, xat(k), z, :, cols], p1_r.at[p, i])
        for k in range(4):
            a, b = (slice(0, 2), slice(2, 4)) if k == 3 else (slice(0, 4),) * 2
            i = 3 + 2 * k
            src = W.at[c, a, zat(-k), :, cols]
            push(src, src, p1_s.at[p, i], p1_r.at[p, i], zdev(1))
            src = W.at[c, b, zat(k), :, cols]
            push(src, src, p1_s.at[p, i + 1], p1_r.at[p, i + 1], zdev(-1))
            yield
            arrived(W.at[c, a, zat(-k - 1), :, cols], p1_r.at[p, i])
            arrived(W.at[c, b, zat(k + 1), :, cols], p1_r.at[p, i + 1])

    def z_then_x(p):
        cols = slice(PHASES[p][1], PHASES[p][2])
        for k in range(4):
            a, b = (slice(0, 16), slice(16, 32)) if k == 3 else (slice(0, 32),) * 2
            i = 2 * k
            src = W.at[c, x, zat(-k), a, cols]
            push(src, src, p2_s.at[p, i], p2_r.at[p, i], zdev(1))
            src = W.at[c, x, zat(k), b, cols]
            push(src, src, p2_s.at[p, i + 1], p2_r.at[p, i + 1], zdev(-1))
            yield
            arrived(W.at[c, x, zat(-k - 1), a, cols], p2_r.at[p, i])
            arrived(W.at[c, x, zat(k + 1), b, cols], p2_r.at[p, i + 1])
        mine = W.at[c, x, :, :, cols]
        push(mine, mine, p2_s.at[p, 8], p2_r.at[p, 8], xdev(1))
        push(mine, mine, p2_s.at[p, 9], p2_r.at[p, 9], xdev(-1))
        yield
        arrived(W.at[c, xat(-1), :, :, cols], p2_r.at[p, 8])
        arrived(W.at[c, xat(1), :, :, cols], p2_r.at[p, 9])
        src = W.at[c, xat(-1), 0:4, :, cols]
        push(src, src, p2_s.at[p, 10], p2_r.at[p, 10], xdev(1))
        src = W.at[c, xat(1), 4:8, :, cols]
        push(src, src, p2_s.at[p, 11], p2_r.at[p, 11], xdev(-1))
        yield
        arrived(W.at[c, xat(2), 0:4, :, cols], p2_r.at[p, 10])
        arrived(W.at[c, xat(2), 4:8, :, cols], p2_r.at[p, 11])

    def share_half(p):
        half = W.at[c, :, :, :, PHASES[p][0] : PHASES[p][2]]
        push(half, half, sib_s.at[p], sib_r.at[p], sibling)

    def half_shared(p):
        arrived(W.at[1 - c, :, :, :, PHASES[p][0] : PHASES[p][2]], sib_r.at[p])

    def normalize():
        @pl.loop(0, TOK // 32)
        def _(i):
            rows = pl.ds(pl.multiple_of(i * 32, 32), 32)
            wide = res[rows, :].astype(F32)
            spread = jnp.mean(wide * wide, axis=-1, keepdims=True)
            nb[rows, :] = (wide * lax.rsqrt(spread + EPS) * gbuf[0:1, :]).astype(BF16)

    def project(first, columns, dst, row0):
        @pl.loop(0, columns // 256)
        def _(i):
            there = pl.ds(pl.multiple_of(first + i * 256, 256), 256)
            w = W[:, :, :, :, there].reshape(D, 256)
            y = jnp.dot(nb[...], w, preferred_element_type=F32)
            dst[row0 : row0 + TOK, pl.ds(pl.multiple_of(i * 256, 256), 256)] = y.astype(BF16)

    halo_to = worker(layer, share + 1)

    def halo_copy():
        return pltpu.make_async_remote_copy(
            kv.at[256:384], kv.at[0:128], halo_s.at[0], halo_r.at[0], device_id=halo_to, device_id_type=MESH
        )

    def keyvals():
        project(0, 1024, kv, 128)
        pl.when(share < 63)(lambda: halo_copy().start())

        def no_prior():
            kv[0:128, :] = jnp.zeros((128, 1024), BF16)

        pl.when(share == 0)(no_prior)

    def attend(j):
        project(1024 + 512 * j, 512, qb, 0)
        key = slice(HD * j, HD * j + HD)
        value = slice(KVD + HD * j, KVD + HD * j + HD)

        @pl.loop(0, 2)
        def _(i):
            b = 1 - i
            rows = pl.ds(pl.multiple_of(b * 128, 128), 128)
            near = pl.ds(pl.multiple_of(b * 128, 128), 256)
            q4 = jnp.concatenate([qb[rows, HD * g : HD * g + HD] for g in range(4)], axis=0)

            def score(keys):
                return SCALE * lax.dot_general(q4, keys, (((1,), (1,)), ((), ())), preferred_element_type=F32)

            s_glob = score(G[0, :, :, key].reshape(256, HD))
            s_rand = score(cbuf[:, key]) + bbuf[pl.ds(b, 1), :]
            at_row = lax.broadcasted_iota(jnp.int32, (512, 256), 0) % 128
            at_col = lax.broadcasted_iota(jnp.int32, (512, 256), 1)
            prior = (at_col < 128) & ((share > 0) | (b > 0))
            own = (at_col >= 128) & (at_col - 128 <= at_row)
            s_near = jnp.where(prior | own, score(kv[near, key]), -jnp.inf)
            top = jnp.maximum(
                jnp.max(s_rand, axis=-1, keepdims=True),
                jnp.max(jnp.maximum(s_glob, s_near), axis=-1, keepdims=True),
            )
            e_glob, e_rand, e_near = jnp.exp2(s_glob - top), jnp.exp2(s_rand - top), jnp.exp2(s_near - top)
            total = jnp.sum(e_rand, axis=-1, keepdims=True) + jnp.sum(e_glob + e_near, axis=-1, keepdims=True)
            heads = jnp.dot(e_glob.astype(BF16), G[1, :, :, key].reshape(256, HD), preferred_element_type=F32)
            heads += jnp.dot(e_rand.astype(BF16), cbuf[:, value], preferred_element_type=F32)
            heads += jnp.dot(e_near.astype(BF16), kv[near, value], preferred_element_type=F32)
            heads = heads / total
            for g in range(4):
                left = res[rows, 512 * j + HD * g : 512 * j + HD * g + HD].astype(F32)
                ob[j, rows, HD * g : HD * g + HD] = (left + heads[128 * g : 128 * g + 128]).astype(BF16)

        push(ob.at[j], out.at[0, :, 512 * j : 512 * j + 512], out_s.at[j], out_r.at[j], target)

    pl.when(is_source)(lambda: scatter(lambda copy: copy.start()))
    pl.when(is_source & (c == 0))(
        lambda: pltpu.make_async_copy(cache.at[0, 0:ROWS, 0:512], G.at[0, 0], gs_r.at[0]).start()
    )
    bring(0, 5)
    brought(0)
    active = [[x_then_z(0), z_then_x(0)]]
    waiting_globals = globals_round()
    done = []

    def tick():
        for p, group in enumerate(active):
            for process in list(group):
                if next(process, 0) == 0:
                    group.remove(process)
            if not group and p not in done:
                done.append(p)
                share_half(p)

    tick()
    bring(5, 9)
    brought(1)
    step = 0
    computed = 0
    globals_running = True
    while len(done) < NP:
        step += 1
        if step % 2 == 0 and len(active) < NP:
            p = len(active)
            active.append([x_then_z(p), z_then_x(p)])
        tick()
        if globals_running:
            globals_running = next(waiting_globals, 0) != 0
        if step == 7:
            brought(2)
            brought(3)
            normalize()
            half_shared(0)
            keyvals()
        if step >= 9 and step % 2 == 1 and computed < NP - 2:
            if computed == 0:
                brought(4)
                brought(5)
                brought(6)
                arrived(G.at[1 - c], gsib_r.at[0])
                pl.when(share > 0)(lambda: arrived(kv.at[0:128], halo_r.at[0]))
            if computed == 2:
                brought(7)
                brought(8)
            half_shared(computed + 1)
            attend(computed)
            computed += 1
    while computed < NP - 1:
        if computed == 2:
            brought(7)
            brought(8)
        half_shared(computed + 1)
        attend(computed)
        computed += 1

    for j in range(4):
        arrived(out.at[0, :, 512 * j : 512 * j + 512], out_r.at[j])
    for copy in sends:
        copy.wait_send()
    pl.when(share < 63)(lambda: halo_copy().wait_send())
    pl.when(is_source)(lambda: scatter(lambda copy: copy.wait_send()))

    def spread_sent():
        for k in range(1, NX):
            pltpu.make_async_remote_copy(
                G.at[c, z], G.at[c, z], gx_s.at[k - 1], gx_r.at[0], device_id=xdev(k), device_id_type=MESH
            ).wait_send()

    pl.when(x == 0)(spread_sent)

    def traded():
        for k in range(9):
            src, dst = entries(yl)[k]
            pltpu.make_async_remote_copy(
                src, dst, in_s.at[k], in_r.at[k], device_id=partner, device_id_type=MESH
            ).wait_send()

    pl.when(swapped)(traded)


def per_device(activations, norm_gain, query_weight, keyval_weight, prefix_cache, random_blocks):
    anywhere = pl.BlockSpec(memory_space=pl.ANY)
    dma = pltpu.SemaphoreType.DMA
    return pl.pallas_call(
        kernel,
        out_shape=jax.ShapeDtypeStruct((1, TOK, D), BF16),
        in_specs=[
            anywhere, pl.BlockSpec(memory_space=pltpu.VMEM), anywhere, anywhere, anywhere,
            pl.BlockSpec(memory_space=pltpu.SMEM),
        ],
        out_specs=anywhere,
        scratch_shapes=[
            pltpu.VMEM((2, NX, NZ, ROWS, 3072), BF16),
            pltpu.VMEM((2, NZ, ROWS, 512), BF16),
            pltpu.VMEM((TOK, D), BF16),
            pltpu.VMEM((TOK, D), BF16),
            pltpu.VMEM((512, 1024), BF16),
            pltpu.VMEM((384, 1024), BF16),
            pltpu.VMEM((TOK, 512), BF16),
            pltpu.VMEM((4, TOK, 512), BF16),
            pltpu.VMEM((8, D), F32),
            pltpu.VMEM((8, D), F32),
            pltpu.VMEM((8, 512), F32),
            pltpu.VMEM((8, 512), F32),
            dma((9,)), dma((9,)),
            dma((16,)), dma((1,)), dma((3,)), dma((1,)), dma((8,)), dma((8,)),
            dma((NP, 11)), dma((NP, 11)), dma((NP, 12)), dma((NP, 12)),
            dma((NP,)), dma((NP,)), dma((1,)), dma((1,)),
            dma((1,)), dma((1,)), dma((4,)), dma((4,)),
        ],
        compiler_params=pltpu.CompilerParams(
            collective_id=0, has_side_effects=True, vmem_limit_bytes=48 * 1024 * 1024
        ),
        cost_estimate=pl.CostEstimate(flops=5 * 10**9, bytes_accessed=2 * 10**7, transcendentals=4 * 10**6),
        name="relay_step",
    )(activations, norm_gain, query_weight, keyval_weight, prefix_cache, random_blocks)


def solution(mesh):
    return jax.shard_map(
        per_device,
        mesh=mesh,
        in_specs=(
            P("section", "dp", None),
            P("section", None),
            P("section", "dp", None),
            P("section", "dp", None),
            P("section", "dp", None),
            P("dp", None),
        ),
        out_specs=P("section", "dp", None),
        check_vma=False,
    )
```

```python
import math

import jax
import jax.numpy as jnp
from jax import lax
from jax.experimental import pallas as pl
from jax.experimental.pallas import tpu as pltpu
from jax.sharding import PartitionSpec as P

KVH = 4
HD = 128
D = 2048
KVD = 512
TOK = 256
NX, NZ = 4, 8
ROWS = 32
EPS = 1e-05
MESH = pl.DeviceIdType.MESH
F32, BF16 = jnp.float32, jnp.bfloat16
SCALE = math.log2(math.e) / math.sqrt(HD)

GROUP = 768
SPLIT = (256, 256, 256, 128)
NTOKENS = 245
ORDER = (
    ("A", 0, 0), ("B", 0, 0), ("A", 1, 0), ("B", 1, 0), ("U", 0, 0), ("B", 0, 1), ("c", 0, 0), ("A", 0, 1),
    ("F", 0, 0), ("B", 1, 1), ("A", 1, 1), ("F", 1, 0), ("B", 0, 2), ("A", 0, 2), ("U", 0, 1), ("B", 1, 2),
    ("F", 0, 1), ("A", 2, 0), ("A", 1, 2), ("B", 2, 0), ("B", 0, 3), ("F", 1, 1), ("F", 0, 2), ("A", 0, 3),
    ("n", 0, 0), ("U", 0, 2), ("B", 1, 3), ("A", 1, 3), ("F", 1, 2), ("A", 2, 1), ("B", 0, 4), ("B", 2, 1),
    ("F", 0, 3), ("A", 0, 4), ("F", 2, 0), ("U", 0, 3), ("B", 1, 4), ("F", 1, 3), ("A", 1, 4), ("A", 3, 0),
    ("B", 3, 0), ("F", 0, 4), ("G", 0, 0), ("A", 2, 2), ("A", 0, 5), ("B", 2, 2), ("U", 0, 4), ("F", 2, 1),
    ("A", 1, 5), ("F", 1, 4), ("G", 1, 0), ("B", 3, 1), ("A", 3, 1), ("F", 3, 0), ("G", 0, 1), ("A", 2, 3),
    ("B", 2, 3), ("U", 0, 5), ("F", 2, 2), ("G", 1, 1), ("B", 3, 2), ("q", 0, 0), ("A", 2, 4), ("B", 2, 4),
    ("F", 2, 3), ("A", 3, 2), ("F", 3, 1), ("B", 3, 3), ("q", 1, 0), ("F", 3, 2), ("F", 2, 4), ("A", 2, 5),
    ("G", 2, 0), ("A", 3, 3), ("B", 3, 4), ("t", 0, 1), ("F", 3, 3), ("t", 0, 0), ("G", 2, 1), ("A", 3, 4),
    ("F", 3, 4), ("G", 3, 0), ("t", 1, 1), ("q", 2, 0), ("A", 3, 5), ("G", 3, 1), ("t", 1, 0), ("t", 2, 1),
    ("q", 3, 0), ("t", 2, 0), ("t", 3, 1), ("t", 3, 0),
)


def kernel(
    act, gain, qw, kvw, cache, rb, out,
    W, G, res, nb, cbuf, kv, qb, ob, gown, gbuf, bown, bbuf,
    in_s, in_r, gs_s, gs_r, gx_s, gx_r, all_s, all_r,
):
    s, d = lax.axis_index("section"), lax.axis_index("dp")
    yh, c = lax.div(s, 2), lax.rem(s, 2)
    yl, xz = lax.div(d, 32), lax.rem(d, 32)
    x, z = lax.div(xz, NZ), lax.rem(xz, NZ)
    base = 32 * yl
    share, layer = 32 * c + xz, 2 * yh + yl
    swapped = c != yl

    def xat(k):
        return lax.rem(x + k + NX, NX)

    def zat(k):
        return lax.rem(z + k + NZ, NZ)

    def xdev(k):
        return (s, base + NZ * xat(k) + z)

    def zdev(k):
        return (s, base + NZ * x + zat(k))

    def worker(layer_, share_):
        return (2 * lax.div(layer_, 2) + lax.div(share_, 32), 32 * lax.rem(layer_, 2) + lax.rem(share_, 32))

    sibling = (2 * yh + 1 - c, d)
    partner = (2 * yh + 1 - c, 32 * (1 - yl) + xz)
    target = (lax.rem(layer + 1, 8), share)
    origin = worker(lax.rem(s + 7, 8), d)
    is_source = d == 0

    bar = pltpu.get_barrier_semaphore()

    def greet(dev):
        pl.semaphore_signal(bar, inc=1, device_id=dev, device_id_type=MESH)

    for dev in (xdev(1), xdev(-1), xdev(2), zdev(1), zdev(-1), sibling, origin):
        greet(dev)
    pl.when(swapped)(lambda: greet(partner))
    pl.when(share > 0)(lambda: greet(worker(layer, share - 1)))
    scattered = (x == 0) & jnp.logical_not((d == 0) & (c == 0))
    pl.when(scattered)(lambda: greet((layer, 0)))

    gown[...] = jnp.broadcast_to(gain[...].astype(F32), (8, D))
    blocks = lax.broadcasted_iota(jnp.int32, (8, 512), 1) // 128 + 4 * d
    row = lax.broadcasted_iota(jnp.int32, (8, 512), 0)
    picked = [
        (blocks == rb[b, 0]) | (blocks == rb[b, 1]) | (blocks == rb[b, 2]) for b in range(2)
    ]
    zero, never = jnp.zeros((8, 512), F32), jnp.full((8, 512), -jnp.inf, F32)
    bown[...] = jnp.where(row == 0, jnp.where(picked[0], zero, never), jnp.where(picked[1], zero, never))

    extra = jnp.where(is_source, 15 + c, 0)
    pl.semaphore_wait(bar, 7 + swapped.astype(jnp.int32) + (share < 63).astype(jnp.int32) + extra)

    sends, tokens, seen = [], {}, set()

    def push(token, src, dev, recv=None, dst=None):
        i = len(tokens)
        tokens[token] = (src if recv is None else recv, i)
        copy = pltpu.make_async_remote_copy(
            src, src if dst is None else dst, all_s.at[i], all_r.at[i], device_id=dev, device_id_type=MESH
        )
        copy.start()
        sends.append(copy)

    def arrived(ref, sem):
        pltpu.make_async_copy(ref, ref, sem).wait()

    def await_token(*names):
        for name in names:
            if name not in seen:
                seen.add(name)
                ref, i = tokens[name]
                arrived(ref, all_r.at[i])

    def entries(slot):
        pairs = []
        for j in range(KVH):
            at = GROUP * j
            for src, first, last in (
                (kvw.at[0, :, HD * j : HD * j + HD], at, at + 128),
                (kvw.at[0, :, KVD + HD * j : KVD + HD * j + HD], at + 128, at + 256),
                (qw.at[0, :, 512 * j : 512 * j + 512], at + 256, at + 768),
            ):
                pairs.append((src, W.at[slot, x, z, :, first:last]))
        pairs += [(gown, gbuf), (act.at[0], res), (bown, bbuf)]
        for j in range(KVH):
            for h in range(2):
                first = KVD * h + HD * j
                pairs.append((cache.at[0, :, first : first + HD], cbuf.at[j, h]))
        return pairs

    def trade_copy(k):
        src, dst = entries(yl)[k]
        return pltpu.make_async_remote_copy(
            src, dst, in_s.at[k], in_r.at[k], device_id=partner, device_id_type=MESH
        )

    def bring(first, last):
        def own():
            for k in range(first, last):
                src, dst = entries(yl)[k]
                pltpu.make_async_copy(src, dst, in_r.at[k]).start()

        def trade():
            for k in range(first, last):
                trade_copy(k).start()

        pl.when(jnp.logical_not(swapped))(own)
        pl.when(swapped)(trade)

    def brought(*which):
        for k in which:
            if k not in seen:
                seen.add(k)
                arrived(entries(c)[k][1], in_r.at[k])

    def scatter_copy(ct, zt):
        return pltpu.make_async_remote_copy(
            cache.at[0, ROWS * zt : ROWS * zt + ROWS, 512 * ct : 512 * ct + 512], G.at[ct, zt],
            gs_s.at[8 * ct + zt], gs_r.at[0],
            device_id=(2 * yh + ct, 32 * c + zt), device_id_type=MESH,
        )

    def scatter(act_on):
        for ct in range(2):
            for zt in range(8):
                if (ct, zt) == (0, 0):
                    pl.when(c == 1)(lambda: act_on(scatter_copy(0, 0)))
                else:
                    act_on(scatter_copy(ct, zt))

    def spread_copy(k):
        return pltpu.make_async_remote_copy(
            G.at[c, z], G.at[c, z], gx_s.at[k - 1], gx_r.at[0], device_id=xdev(k), device_id_type=MESH
        )

    def spread(act_on):
        for k in range(1, NX):
            act_on(spread_copy(k))

    def halves(k, size):
        return (slice(0, size // 2), slice(size // 2, size)) if k == 3 else (slice(0, size),) * 2

    def ring(tag, k, block, size):
        a, b = halves(k, size)
        push((tag, "r", k + 1), block(zat(-k), a), zdev(1), block(zat(-k - 1), a))
        push((tag, "l", k + 1), block(zat(k), b), zdev(-1), block(zat(k + 1), b))

    def step_u(_, k):
        def block(at, part):
            return G.at[c, at, part]

        if k == 0:
            pl.when(x == 0)(lambda: arrived(G.at[c, z], gs_r.at[0]))
            pl.when(x == 0)(lambda: spread(lambda copy: copy.start()))
            return
        k -= 1
        if k == 0:
            pl.when(x != 0)(lambda: arrived(G.at[c, z], gx_r.at[0]))
        else:
            await_token(("U", "r", k), ("U", "l", k))
        if k < 4:
            ring("U", k, block, 32)
        else:
            push("Us", G.at[c], sibling, G.at[1 - c])

    def columns_a(p):
        return slice(GROUP * p, GROUP * p + SPLIT[p])

    def columns_b(p):
        return slice(GROUP * p + SPLIT[p], GROUP * (p + 1))

    def offsets(k):
        return (0,) if k == 0 else (4,) if k == 4 else (-k, k)

    def step_a(p, k):
        cols = columns_a(p)

        def block(at, part):
            return W.at[c, part, at, :, cols]

        if k == 0:
            brought(3 * p, 3 * p + 1, 3 * p + 2)
            for i in (1, -1, 2):
                push(("A", p, "x", i), W.at[c, x, z, :, cols], xdev(i), W.at[c, xat(-i), z, :, cols])
            return
        k -= 1
        if k == 0:
            await_token(*(("A", p, "x", i) for i in (1, -1, 2)))
        else:
            await_token((("A", p), "r", k), (("A", p), "l", k))
        if k < 4:
            ring(("A", p), k, block, 4)
        for q in offsets(k):
            push(("A", p, "s", q), W.at[c, :, zat(q), :, cols], sibling, W.at[1 - c, :, zat(q), :, cols])

    def hand_b(p, i, xo):
        cols = columns_b(p)
        push(("B", p, "s", i), W.at[c, xat(xo), :, :, cols], sibling, W.at[1 - c, xat(xo), :, :, cols])

    def step_b(p, k):
        cols = columns_b(p)

        def block(at, part):
            return W.at[c, x, at, part, cols]

        if k == 0:
            brought(3 * p, 3 * p + 1, 3 * p + 2)
        else:
            await_token((("B", p), "r", k), (("B", p), "l", k))
        if k < 4:
            ring(("B", p), k, block, 32)
        for q in offsets(k):
            mine = W.at[c, x, zat(q), :, cols]
            push(("B", p, "a", q), mine, xdev(1), W.at[c, xat(-1), zat(q), :, cols])
            push(("B", p, "b", q), mine, xdev(-1), W.at[c, xat(1), zat(q), :, cols])
        if k == 4:
            hand_b(p, 0, 0)

    def step_f(p, k):
        cols = columns_b(p)

        def along(xo, q, part):
            return W.at[c, xat(xo), zat(q), part, cols]

        await_token(*(("B", p, way, q) for way in "ab" for q in offsets(k)))
        if k in (0, 4):
            up, down, qa, qb_ = slice(0, 16), slice(16, 32), k, k
        else:
            up, down, qa, qb_ = slice(0, 32), slice(0, 32), -k, k
        push(("F", p, "a", k), along(-1, qa, up), xdev(1), along(2, qa, up))
        push(("F", p, "b", k), along(1, qb_, down), xdev(-1), along(2, qb_, down))

    def step_g(p, k):
        if k == 0:
            await_token(*(("B", p, way, q) for way in "ab" for q in range(-3, 5)))
            hand_b(p, 1, -1)
            hand_b(p, 2, 1)
        else:
            await_token(*(("F", p, way, q) for way in "ab" for q in range(5)))
            hand_b(p, 3, 2)

    def half_shared(p):
        if SPLIT[p]:
            await_token(*(("A", p, "s", q) for q in range(-3, 5)))
        if SPLIT[p] < GROUP:
            await_token(*(("B", p, "s", i) for i in range(4)))

    def step_c(*_):
        bring(15, 23)

    def step_n(*_):
        brought(12, 13)

        @pl.loop(0, TOK // 32)
        def _(i):
            rows = pl.ds(pl.multiple_of(i * 32, 32), 32)
            wide = res[rows, :].astype(F32)
            spread_ = jnp.mean(wide * wide, axis=-1, keepdims=True)
            nb[rows, :] = (wide * lax.rsqrt(spread_ + EPS) * gbuf[0:1, :]).astype(BF16)

    halo_to = worker(layer, share + 1)

    def halo_copy(j):
        cols = slice(256 * j, 256 * j + 256)
        return pltpu.make_async_remote_copy(
            kv.at[256:384, cols], kv.at[0:128, cols], in_s.at[23 + j], in_r.at[23 + j],
            device_id=halo_to, device_id_type=MESH,
        )

    def step_q(j, _):
        half_shared(j)

        def times(first):
            w = W[:, :, :, :, GROUP * j + first : GROUP * j + first + 256].reshape(D, 256)
            return jnp.dot(nb[...], w, preferred_element_type=F32).astype(BF16)

        kv[128:384, 256 * j : 256 * j + 256] = times(0)
        pl.when(share < 63)(lambda: halo_copy(j).start())
        qb[j, :, 0:256] = times(256)
        qb[j, :, 256:512] = times(512)

    def step_t(j, b):
        brought(14, 15 + 2 * j, 16 + 2 * j)
        await_token("Us")
        if b == 0:
            pl.when(share > 0)(lambda: arrived(kv.at[0:128, 256 * j : 256 * j + 256], in_r.at[23 + j]))
        key = slice(HD * j, HD * j + HD)
        rows = slice(128 * b, 128 * b + 128)
        near = slice(128 * b, 128 * b + 256)
        near_key, near_value = slice(256 * j, 256 * j + 128), slice(256 * j + 128, 256 * j + 256)
        q4 = jnp.concatenate([qb[j, rows, HD * g : HD * g + HD] for g in range(4)], axis=0)

        def score(keys):
            return SCALE * lax.dot_general(q4, keys, (((1,), (1,)), ((), ())), preferred_element_type=F32)

        s_glob = score(G[0, :, :, key].reshape(256, HD))
        s_rand = score(cbuf[j, 0]) + bbuf[b : b + 1, :]
        at_row = lax.broadcasted_iota(jnp.int32, (512, 256), 0) % 128
        at_col = lax.broadcasted_iota(jnp.int32, (512, 256), 1)
        prior = at_col < 128
        if b == 0:
            prior = prior & (share > 0)
        own = (at_col >= 128) & (at_col - 128 <= at_row)
        s_near = jnp.where(prior | own, score(kv[near, near_key]), -jnp.inf)
        top = jnp.maximum(
            jnp.max(s_rand, axis=-1, keepdims=True),
            jnp.max(jnp.maximum(s_glob, s_near), axis=-1, keepdims=True),
        )
        e_glob, e_rand, e_near = jnp.exp2(s_glob - top), jnp.exp2(s_rand - top), jnp.exp2(s_near - top)
        total = jnp.sum(e_rand, axis=-1, keepdims=True) + jnp.sum(e_glob + e_near, axis=-1, keepdims=True)
        heads = jnp.dot(e_glob.astype(BF16), G[1, :, :, key].reshape(256, HD), preferred_element_type=F32)
        heads += jnp.dot(e_rand.astype(BF16), cbuf[j, 1], preferred_element_type=F32)
        heads += jnp.dot(e_near.astype(BF16), kv[near, near_value], preferred_element_type=F32)
        heads = heads / total
        for g in range(4):
            left = res[rows, 512 * j + HD * g : 512 * j + HD * g + HD].astype(F32)
            ob[j, rows, HD * g : HD * g + HD] = (left + heads[128 * g : 128 * g + 128]).astype(BF16)
        there = out.at[0, rows, 512 * j : 512 * j + 512]
        push(("o", j, b), ob.at[j, rows], target, there, there)

    pl.when(is_source)(lambda: scatter(lambda copy: copy.start()))
    pl.when(is_source & (c == 0))(
        lambda: pltpu.make_async_copy(cache.at[0, 0:ROWS, 0:512], G.at[0, 0], gs_r.at[0]).start()
    )
    bring(0, 15)

    def no_prior():
        kv[0:128, :] = jnp.zeros((128, 1024), BF16)

    pl.when(share == 0)(no_prior)
    steps = dict(
        A=step_a, B=step_b, F=step_f, G=step_g, U=step_u, c=step_c, n=step_n, q=step_q, t=step_t
    )
    for name, p, k in ORDER:
        steps[name](p, k)

    await_token(*(("o", j, b) for j in range(KVH) for b in range(2)))
    for copy in sends:
        copy.wait_send()
    for j in range(KVH):
        pl.when(share < 63)(lambda j=j: halo_copy(j).wait_send())
    pl.when(is_source)(lambda: scatter(lambda copy: copy.wait_send()))
    pl.when(x == 0)(lambda: spread(lambda copy: copy.wait_send()))

    def traded():
        for k in range(23):
            trade_copy(k).wait_send()

    pl.when(swapped)(traded)


def per_device(activations, norm_gain, query_weight, keyval_weight, prefix_cache, random_blocks):
    anywhere = pl.BlockSpec(memory_space=pl.ANY)
    dma = pltpu.SemaphoreType.DMA
    return pl.pallas_call(
        kernel,
        out_shape=jax.ShapeDtypeStruct((1, TOK, D), BF16),
        in_specs=[
            anywhere, pl.BlockSpec(memory_space=pltpu.VMEM), anywhere, anywhere, anywhere,
            pl.BlockSpec(memory_space=pltpu.SMEM),
        ],
        out_specs=anywhere,
        scratch_shapes=[
            pltpu.VMEM((2, NX, NZ, ROWS, 3072), BF16),
            pltpu.VMEM((2, NZ, ROWS, 512), BF16),
            pltpu.VMEM((TOK, D), BF16),
            pltpu.VMEM((TOK, D), BF16),
            pltpu.VMEM((4, 2, 512, HD), BF16),
            pltpu.VMEM((384, 1024), BF16),
            pltpu.VMEM((4, TOK, 512), BF16),
            pltpu.VMEM((4, TOK, 512), BF16),
            pltpu.VMEM((8, D), F32),
            pltpu.VMEM((8, D), F32),
            pltpu.VMEM((8, 512), F32),
            pltpu.VMEM((8, 512), F32),
            dma((27,)), dma((27,)),
            dma((16,)), dma((1,)), dma((3,)), dma((1,)), dma((NTOKENS,)), dma((NTOKENS,)),
        ],
        compiler_params=pltpu.CompilerParams(
            collective_id=0, has_side_effects=True, vmem_limit_bytes=60 * 1024 * 1024
        ),
        cost_estimate=pl.CostEstimate(flops=5 * 10**9, bytes_accessed=2 * 10**7, transcendentals=4 * 10**6),
        name="relay_step",
    )(activations, norm_gain, query_weight, keyval_weight, prefix_cache, random_blocks)


def solution(mesh):
    return jax.shard_map(
        per_device,
        mesh=mesh,
        in_specs=(
            P("section", "dp", None),
            P("section", None),
            P("section", "dp", None),
            P("section", "dp", None),
            P("section", "dp", None),
            P("dp", None),
        ),
        out_specs=P("section", "dp", None),
        check_vma=False,
    )
```

```python
import math

import jax
import jax.numpy as jnp
from jax import lax
from jax.experimental import pallas as pl
from jax.experimental.pallas import tpu as pltpu
from jax.sharding import PartitionSpec as P

KVH = 4
HD = 128
D = 2048
KVD = 512
TOK = 256
NX, NZ = 4, 8
ROWS = 32
EPS = 1e-05
MESH = pl.DeviceIdType.MESH
F32, BF16 = jnp.float32, jnp.bfloat16
SCALE = math.log2(math.e) / math.sqrt(HD)

GROUP = 768
SPLIT = (256, 256, 384, 128)
NTOKENS = 217
ORDER = (
    ("A", 0, 0), ("B", 0, 0), ("A", 1, 0), ("B", 1, 0), ("U", 0, 0), ("B", 0, 1), ("c", 0, 0), ("A", 0, 1),
    ("F", 0, 0), ("B", 1, 1), ("A", 1, 1), ("F", 1, 0), ("B", 0, 2), ("U", 0, 1), ("A", 0, 2), ("B", 1, 2),
    ("F", 0, 1), ("A", 1, 2), ("F", 1, 1), ("B", 0, 3), ("A", 2, 0), ("B", 2, 0), ("U", 0, 2), ("F", 0, 2),
    ("n", 0, 0), ("A", 0, 3), ("B", 1, 3), ("F", 1, 2), ("A", 1, 3), ("B", 0, 4), ("B", 2, 1), ("F", 0, 3),
    ("U", 0, 3), ("A", 3, 0), ("B", 3, 0), ("A", 2, 1), ("A", 0, 4), ("B", 1, 4), ("F", 2, 0), ("A", 1, 4),
    ("F", 1, 3), ("B", 2, 2), ("U", 0, 4), ("F", 0, 4), ("G", 0, 0), ("B", 3, 1), ("F", 2, 1), ("A", 2, 2),
    ("A", 3, 1), ("F", 3, 0), ("A", 0, 5), ("F", 1, 4), ("A", 1, 5), ("G", 1, 0), ("U", 0, 5), ("B", 2, 3),
    ("B", 3, 2), ("G", 0, 1), ("F", 2, 2), ("A", 2, 3), ("F", 3, 1), ("A", 3, 2), ("B", 2, 4), ("G", 1, 1),
    ("B", 3, 3), ("F", 2, 3), ("q", 0, 0), ("F", 3, 2), ("q", 1, 0), ("A", 2, 4), ("F", 2, 4), ("G", 2, 0),
    ("A", 3, 3), ("B", 3, 4), ("F", 3, 3), ("t", 0, 1), ("t", 1, 1), ("A", 2, 5), ("G", 2, 1), ("F", 3, 4),
    ("A", 3, 4), ("G", 3, 0), ("t", 0, 0), ("t", 1, 0), ("A", 3, 5), ("G", 3, 1), ("q", 2, 0), ("t", 2, 1),
    ("q", 3, 0), ("t", 3, 1), ("t", 2, 0), ("t", 3, 0),
)


def kernel(
    act, gain, qw, kvw, cache, rb, out,
    W, G, res, nb, cbuf, kv, qb, ob, gown, gbuf, bown, bbuf,
    in_s, in_r, gs_s, gs_r, gx_s, gx_r, all_s, all_r,
):
    s, d = lax.axis_index("section"), lax.axis_index("dp")
    yh, c = lax.div(s, 2), lax.rem(s, 2)
    yl, xz = lax.div(d, 32), lax.rem(d, 32)
    x, z = lax.div(xz, NZ), lax.rem(xz, NZ)
    base = 32 * yl
    share, layer = 32 * c + xz, 2 * yh + yl
    swapped = c != yl

    def xat(k):
        return lax.rem(x + k + NX, NX)

    def zat(k):
        return lax.rem(z + k + NZ, NZ)

    def xdev(k):
        return (s, base + NZ * xat(k) + z)

    def zdev(k):
        return (s, base + NZ * x + zat(k))

    def worker(layer_, share_):
        return (2 * lax.div(layer_, 2) + lax.div(share_, 32), 32 * lax.rem(layer_, 2) + lax.rem(share_, 32))

    sibling = (2 * yh + 1 - c, d)
    partner = (2 * yh + 1 - c, 32 * (1 - yl) + xz)
    target = (lax.rem(layer + 1, 8), share)
    origin = worker(lax.rem(s + 7, 8), d)
    is_source = d == 0

    bar = pltpu.get_barrier_semaphore()

    def greet(dev):
        pl.semaphore_signal(bar, inc=1, device_id=dev, device_id_type=MESH)

    for dev in (xdev(1), xdev(-1), xdev(2), zdev(1), zdev(-1), sibling, origin):
        greet(dev)
    pl.when(swapped)(lambda: greet(partner))
    pl.when(share > 0)(lambda: greet(worker(layer, share - 1)))
    scattered = (x == 0) & jnp.logical_not((d == 0) & (c == 0))
    pl.when(scattered)(lambda: greet((layer, 0)))

    gown[...] = jnp.broadcast_to(gain[...].astype(F32), (8, D))
    blocks = lax.broadcasted_iota(jnp.int32, (8, 512), 1) // 128 + 4 * d
    row = lax.broadcasted_iota(jnp.int32, (8, 512), 0)
    picked = [
        (blocks == rb[b, 0]) | (blocks == rb[b, 1]) | (blocks == rb[b, 2]) for b in range(2)
    ]
    zero, never = jnp.zeros((8, 512), F32), jnp.full((8, 512), -jnp.inf, F32)
    bown[...] = jnp.where(row == 0, jnp.where(picked[0], zero, never), jnp.where(picked[1], zero, never))

    extra = jnp.where(is_source, 15 + c, 0)
    pl.semaphore_wait(bar, 7 + swapped.astype(jnp.int32) + (share < 63).astype(jnp.int32) + extra)

    sends, tokens, seen = [], {}, set()

    def push(token, src, dev, recv=None, dst=None):
        i = len(tokens)
        tokens[token] = (src if recv is None else recv, i)
        copy = pltpu.make_async_remote_copy(
            src, src if dst is None else dst, all_s.at[i], all_r.at[i], device_id=dev, device_id_type=MESH
        )
        copy.start()
        sends.append(copy)

    def arrived(ref, sem):
        pltpu.make_async_copy(ref, ref, sem).wait()

    def await_token(*names):
        for name in names:
            if name not in seen:
                seen.add(name)
                ref, i = tokens[name]
                arrived(ref, all_r.at[i])

    def entries(slot):
        pairs = []
        for j in range(KVH):
            at = GROUP * j
            for src, first, last in (
                (kvw.at[0, :, HD * j : HD * j + HD], at, at + 128),
                (kvw.at[0, :, KVD + HD * j : KVD + HD * j + HD], at + 128, at + 256),
                (qw.at[0, :, 512 * j : 512 * j + 512], at + 256, at + 768),
            ):
                pairs.append((src, W.at[slot, x, z, :, first:last]))
        pairs += [(gown, gbuf), (act.at[0], res), (bown, bbuf)]
        for j in range(KVH):
            for h in range(2):
                first = KVD * h + HD * j
                pairs.append((cache.at[0, :, first : first + HD], cbuf.at[j, h]))
        return pairs

    def trade_copy(k):
        src, dst = entries(yl)[k]
        return pltpu.make_async_remote_copy(
            src, dst, in_s.at[k], in_r.at[k], device_id=partner, device_id_type=MESH
        )

    def bring(first, last):
        def own():
            for k in range(first, last):
                src, dst = entries(yl)[k]
                pltpu.make_async_copy(src, dst, in_r.at[k]).start()

        def trade():
            for k in range(first, last):
                trade_copy(k).start()

        pl.when(jnp.logical_not(swapped))(own)
        pl.when(swapped)(trade)

    def brought(*which):
        for k in which:
            if k not in seen:
                seen.add(k)
                arrived(entries(c)[k][1], in_r.at[k])

    def scatter_copy(ct, zt):
        return pltpu.make_async_remote_copy(
            cache.at[0, ROWS * zt : ROWS * zt + ROWS, 512 * ct : 512 * ct + 512], G.at[ct, zt],
            gs_s.at[8 * ct + zt], gs_r.at[0],
            device_id=(2 * yh + ct, 32 * c + zt), device_id_type=MESH,
        )

    def scatter(act_on):
        for ct in range(2):
            for zt in range(8):
                if (ct, zt) == (0, 0):
                    pl.when(c == 1)(lambda: act_on(scatter_copy(0, 0)))
                else:
                    act_on(scatter_copy(ct, zt))

    def spread_copy(k):
        return pltpu.make_async_remote_copy(
            G.at[c, z], G.at[c, z], gx_s.at[k - 1], gx_r.at[0], device_id=xdev(k), device_id_type=MESH
        )

    def spread(act_on):
        for k in range(1, NX):
            act_on(spread_copy(k))

    def halves(k, size):
        return (slice(0, size // 2), slice(size // 2, size)) if k == 3 else (slice(0, size),) * 2

    def ring(tag, k, block, size):
        a, b = halves(k, size)
        push((tag, "r", k + 1), block(zat(-k), a), zdev(1), block(zat(-k - 1), a))
        push((tag, "l", k + 1), block(zat(k), b), zdev(-1), block(zat(k + 1), b))

    def step_u(_, k):
        def block(at, part):
            return G.at[c, at, part]

        if k == 0:
            pl.when(x == 0)(lambda: arrived(G.at[c, z], gs_r.at[0]))
            pl.when(x == 0)(lambda: spread(lambda copy: copy.start()))
            return
        k -= 1
        if k == 0:
            pl.when(x != 0)(lambda: arrived(G.at[c, z], gx_r.at[0]))
        else:
            await_token(("U", "r", k), ("U", "l", k))
        if k < 4:
            ring("U", k, block, 32)
        else:
            push("Us", G.at[c], sibling, G.at[1 - c])

    def columns_a(p):
        return slice(GROUP * p, GROUP * p + SPLIT[p])

    def columns_b(p):
        return slice(GROUP * p + SPLIT[p], GROUP * (p + 1))

    def offsets(k):
        return (0,) if k == 0 else (4,) if k == 4 else (-k, k)

    def step_a(p, k):
        cols = columns_a(p)

        def block(at, part):
            return W.at[c, part, at, :, cols]

        if k == 0:
            brought(3 * p, 3 * p + 1, 3 * p + 2)
            for i in (1, -1, 2):
                push(("A", p, "x", i), W.at[c, x, z, :, cols], xdev(i), W.at[c, xat(-i), z, :, cols])
            return
        k -= 1
        if k == 0:
            await_token(*(("A", p, "x", i) for i in (1, -1, 2)))
        else:
            await_token((("A", p), "r", k), (("A", p), "l", k))
        if k < 4:
            ring(("A", p), k, block, 4)
        else:
            push(("A", p, "s"), W.at[c, :, :, :, cols], sibling, W.at[1 - c, :, :, :, cols])

    def hand_b(p, i, xo):
        cols = columns_b(p)
        push(("B", p, "s", i), W.at[c, xat(xo), :, :, cols], sibling, W.at[1 - c, xat(xo), :, :, cols])

    def step_b(p, k):
        cols = columns_b(p)

        def block(at, part):
            return W.at[c, x, at, part, cols]

        if k == 0:
            brought(3 * p, 3 * p + 1, 3 * p + 2)
        else:
            await_token((("B", p), "r", k), (("B", p), "l", k))
        if k < 4:
            ring(("B", p), k, block, 32)
        for q in offsets(k):
            mine = W.at[c, x, zat(q), :, cols]
            push(("B", p, "a", q), mine, xdev(1), W.at[c, xat(-1), zat(q), :, cols])
            push(("B", p, "b", q), mine, xdev(-1), W.at[c, xat(1), zat(q), :, cols])
        if k == 4:
            hand_b(p, 0, 0)

    def step_f(p, k):
        cols = columns_b(p)

        def along(xo, q, part):
            return W.at[c, xat(xo), zat(q), part, cols]

        await_token(*(("B", p, way, q) for way in "ab" for q in offsets(k)))
        if k in (0, 4):
            up, down, qa, qb_ = slice(0, 16), slice(16, 32), k, k
        else:
            up, down, qa, qb_ = slice(0, 32), slice(0, 32), -k, k
        push(("F", p, "a", k), along(-1, qa, up), xdev(1), along(2, qa, up))
        push(("F", p, "b", k), along(1, qb_, down), xdev(-1), along(2, qb_, down))

    def step_g(p, k):
        if k == 0:
            await_token(*(("B", p, way, q) for way in "ab" for q in range(-3, 5)))
            hand_b(p, 1, -1)
            hand_b(p, 2, 1)
        else:
            await_token(*(("F", p, way, q) for way in "ab" for q in range(5)))
            hand_b(p, 3, 2)

    def half_shared(p):
        if SPLIT[p]:
            await_token(("A", p, "s"))
        if SPLIT[p] < GROUP:
            await_token(*(("B", p, "s", i) for i in range(4)))

    def step_c(*_):
        bring(15, 23)

    def step_n(*_):
        brought(12, 13)

        @pl.loop(0, TOK // 32)
        def _(i):
            rows = pl.ds(pl.multiple_of(i * 32, 32), 32)
            wide = res[rows, :].astype(F32)
            spread_ = jnp.mean(wide * wide, axis=-1, keepdims=True)
            nb[rows, :] = (wide * lax.rsqrt(spread_ + EPS) * gbuf[0:1, :]).astype(BF16)

    halo_to = worker(layer, share + 1)

    def halo_copy(j):
        cols = slice(256 * j, 256 * j + 256)
        return pltpu.make_async_remote_copy(
            kv.at[256:384, cols], kv.at[0:128, cols], in_s.at[23 + j], in_r.at[23 + j],
            device_id=halo_to, device_id_type=MESH,
        )

    def step_q(j, _):
        half_shared(j)

        def times(first):
            w = W[:, :, :, :, GROUP * j + first : GROUP * j + first + 256].reshape(D, 256)
            return jnp.dot(nb[...], w, preferred_element_type=F32).astype(BF16)

        kv[128:384, 256 * j : 256 * j + 256] = times(0)
        pl.when(share < 63)(lambda: halo_copy(j).start())
        qb[j, :, 0:256] = times(256)
        qb[j, :, 256:512] = times(512)

    def step_t(j, b):
        brought(14, 15 + 2 * j, 16 + 2 * j)
        await_token("Us")
        if b == 0:
            pl.when(share > 0)(lambda: arrived(kv.at[0:128, 256 * j : 256 * j + 256], in_r.at[23 + j]))
        key = slice(HD * j, HD * j + HD)
        rows = slice(128 * b, 128 * b + 128)
        near = slice(128 * b, 128 * b + 256)
        near_key, near_value = slice(256 * j, 256 * j + 128), slice(256 * j + 128, 256 * j + 256)
        q4 = jnp.concatenate([qb[j, rows, HD * g : HD * g + HD] for g in range(4)], axis=0)

        def score(keys):
            return SCALE * lax.dot_general(q4, keys, (((1,), (1,)), ((), ())), preferred_element_type=F32)

        s_glob = score(G[0, :, :, key].reshape(256, HD))
        s_rand = score(cbuf[j, 0]) + bbuf[b : b + 1, :]
        at_row = lax.broadcasted_iota(jnp.int32, (512, 256), 0) % 128
        at_col = lax.broadcasted_iota(jnp.int32, (512, 256), 1)
        prior = at_col < 128
        if b == 0:
            prior = prior & (share > 0)
        own = (at_col >= 128) & (at_col - 128 <= at_row)
        s_near = jnp.where(prior | own, score(kv[near, near_key]), -jnp.inf)
        top = jnp.maximum(
            jnp.max(s_rand, axis=-1, keepdims=True),
            jnp.max(jnp.maximum(s_glob, s_near), axis=-1, keepdims=True),
        )
        e_glob, e_rand, e_near = jnp.exp2(s_glob - top), jnp.exp2(s_rand - top), jnp.exp2(s_near - top)
        total = jnp.sum(e_rand, axis=-1, keepdims=True) + jnp.sum(e_glob + e_near, axis=-1, keepdims=True)
        heads = jnp.dot(e_glob.astype(BF16), G[1, :, :, key].reshape(256, HD), preferred_element_type=F32)
        heads += jnp.dot(e_rand.astype(BF16), cbuf[j, 1], preferred_element_type=F32)
        heads += jnp.dot(e_near.astype(BF16), kv[near, near_value], preferred_element_type=F32)
        heads = heads / total
        for g in range(4):
            left = res[rows, 512 * j + HD * g : 512 * j + HD * g + HD].astype(F32)
            ob[j, rows, HD * g : HD * g + HD] = (left + heads[128 * g : 128 * g + 128]).astype(BF16)
        there = out.at[0, rows, 512 * j : 512 * j + 512]
        push(("o", j, b), ob.at[j, rows], target, there, there)

    pl.when(is_source)(lambda: scatter(lambda copy: copy.start()))
    pl.when(is_source & (c == 0))(
        lambda: pltpu.make_async_copy(cache.at[0, 0:ROWS, 0:512], G.at[0, 0], gs_r.at[0]).start()
    )
    bring(0, 15)

    def no_prior():
        kv[0:128, :] = jnp.zeros((128, 1024), BF16)

    pl.when(share == 0)(no_prior)
    steps = dict(
        A=step_a, B=step_b, F=step_f, G=step_g, U=step_u, c=step_c, n=step_n, q=step_q, t=step_t
    )
    for name, p, k in ORDER:
        steps[name](p, k)

    await_token(*(("o", j, b) for j in range(KVH) for b in range(2)))
    for copy in sends:
        copy.wait_send()
    for j in range(KVH):
        pl.when(share < 63)(lambda j=j: halo_copy(j).wait_send())
    pl.when(is_source)(lambda: scatter(lambda copy: copy.wait_send()))
    pl.when(x == 0)(lambda: spread(lambda copy: copy.wait_send()))

    def traded():
        for k in range(23):
            trade_copy(k).wait_send()

    pl.when(swapped)(traded)


def per_device(activations, norm_gain, query_weight, keyval_weight, prefix_cache, random_blocks):
    anywhere = pl.BlockSpec(memory_space=pl.ANY)
    dma = pltpu.SemaphoreType.DMA
    return pl.pallas_call(
        kernel,
        out_shape=pltpu.VMEM((1, TOK, D), BF16),
        in_specs=[
            anywhere, pl.BlockSpec(memory_space=pltpu.VMEM), anywhere, anywhere, anywhere,
            pl.BlockSpec(memory_space=pltpu.SMEM),
        ],
        out_specs=pl.BlockSpec(memory_space=pltpu.VMEM),
        scratch_shapes=[
            pltpu.VMEM((2, NX, NZ, ROWS, 3072), BF16),
            pltpu.VMEM((2, NZ, ROWS, 512), BF16),
            pltpu.VMEM((TOK, D), BF16),
            pltpu.VMEM((TOK, D), BF16),
            pltpu.VMEM((4, 2, 512, HD), BF16),
            pltpu.VMEM((384, 1024), BF16),
            pltpu.VMEM((4, TOK, 512), BF16),
            pltpu.VMEM((4, TOK, 512), BF16),
            pltpu.VMEM((8, D), F32),
            pltpu.VMEM((8, D), F32),
            pltpu.VMEM((8, 512), F32),
            pltpu.VMEM((8, 512), F32),
            dma((27,)), dma((27,)),
            dma((16,)), dma((1,)), dma((3,)), dma((1,)), dma((NTOKENS,)), dma((NTOKENS,)),
        ],
        compiler_params=pltpu.CompilerParams(
            collective_id=0, has_side_effects=True, vmem_limit_bytes=60 * 1024 * 1024
        ),
        cost_estimate=pl.CostEstimate(flops=5 * 10**9, bytes_accessed=2 * 10**7, transcendentals=4 * 10**6),
        name="relay_step",
    )(activations, norm_gain, query_weight, keyval_weight, prefix_cache, random_blocks)


def solution(mesh):
    return jax.shard_map(
        per_device,
        mesh=mesh,
        in_specs=(
            P("section", "dp", None),
            P("section", None),
            P("section", "dp", None),
            P("section", "dp", None),
            P("section", "dp", None),
            P("dp", None),
        ),
        out_specs=P("section", "dp", None),
        check_vma=False,
    )
```

```python
import math

import jax
import jax.numpy as jnp
from jax import lax
from jax.experimental import pallas as pl
from jax.experimental.pallas import tpu as pltpu
from jax.sharding import PartitionSpec as P

KVH = 4
HD = 128
D = 2048
KVD = 512
TOK = 256
NX, NZ = 4, 8
ROWS = 32
EPS = 1e-05
MESH = pl.DeviceIdType.MESH
F32, BF16 = jnp.float32, jnp.bfloat16
SCALE = math.log2(math.e) / math.sqrt(HD)

GROUP = 768
SPLIT = (256, 256, 384, 128)
NTOKENS = 217
ORDER = (
    ("A", 0, 0), ("B", 0, 0), ("A", 1, 0), ("B", 1, 0), ("U", 0, 0), ("B", 0, 1), ("c", 0, 0), ("A", 0, 1),
    ("F", 0, 0), ("B", 1, 1), ("A", 1, 1), ("F", 1, 0), ("B", 0, 2), ("U", 0, 1), ("A", 0, 2), ("B", 1, 2),
    ("F", 0, 1), ("A", 1, 2), ("F", 1, 1), ("B", 0, 3), ("A", 2, 0), ("B", 2, 0), ("U", 0, 2), ("F", 0, 2),
    ("n", 0, 0), ("A", 0, 3), ("B", 1, 3), ("F", 1, 2), ("A", 1, 3), ("B", 0, 4), ("B", 2, 1), ("F", 0, 3),
    ("U", 0, 3), ("A", 3, 0), ("B", 3, 0), ("A", 2, 1), ("A", 0, 4), ("B", 1, 4), ("F", 2, 0), ("A", 1, 4),
    ("F", 1, 3), ("B", 2, 2), ("U", 0, 4), ("F", 0, 4), ("G", 0, 0), ("B", 3, 1), ("F", 2, 1), ("A", 2, 2),
    ("A", 3, 1), ("F", 3, 0), ("A", 0, 5), ("F", 1, 4), ("A", 1, 5), ("G", 1, 0), ("U", 0, 5), ("B", 2, 3),
    ("B", 3, 2), ("G", 0, 1), ("F", 2, 2), ("A", 2, 3), ("F", 3, 1), ("A", 3, 2), ("B", 2, 4), ("G", 1, 1),
    ("B", 3, 3), ("F", 2, 3), ("q", 0, 0), ("F", 3, 2), ("q", 1, 0), ("A", 2, 4), ("F", 2, 4), ("G", 2, 0),
    ("A", 3, 3), ("B", 3, 4), ("F", 3, 3), ("t", 0, 1), ("t", 1, 1), ("A", 2, 5), ("G", 2, 1), ("F", 3, 4),
    ("A", 3, 4), ("G", 3, 0), ("t", 0, 0), ("t", 1, 0), ("A", 3, 5), ("G", 3, 1), ("q", 2, 0), ("t", 2, 1),
    ("q", 3, 0), ("t", 3, 1), ("t", 2, 0), ("t", 3, 0),
)


def kernel(
    act, gain, qw, kvw, cache, rb, out,
    W, G, res, nb, cbuf, kv, qb, ob, gown, gbuf, bown, bbuf,
    in_s, in_r, gs_s, gs_r, gx_s, gx_r, all_s, all_r,
):
    s, d = lax.axis_index("section"), lax.axis_index("dp")
    yh, c = lax.div(s, 2), lax.rem(s, 2)
    yl, xz = lax.div(d, 32), lax.rem(d, 32)
    x, z = lax.div(xz, NZ), lax.rem(xz, NZ)
    base = 32 * yl
    share, layer = 32 * c + xz, 2 * yh + yl
    swapped = c != yl

    def xat(k):
        return lax.rem(x + k + NX, NX)

    def zat(k):
        return lax.rem(z + k + NZ, NZ)

    def xdev(k):
        return (s, base + NZ * xat(k) + z)

    def zdev(k):
        return (s, base + NZ * x + zat(k))

    def worker(layer_, share_):
        return (2 * lax.div(layer_, 2) + lax.div(share_, 32), 32 * lax.rem(layer_, 2) + lax.rem(share_, 32))

    sibling = (2 * yh + 1 - c, d)
    partner = (2 * yh + 1 - c, 32 * (1 - yl) + xz)
    target = (lax.rem(layer + 1, 8), share)
    origin = worker(lax.rem(s + 7, 8), d)
    is_source = d == 0

    bar = pltpu.get_barrier_semaphore()

    def greet(dev):
        pl.semaphore_signal(bar, inc=1, device_id=dev, device_id_type=MESH)

    for dev in (xdev(1), xdev(-1), xdev(2), zdev(1), zdev(-1), sibling, origin):
        greet(dev)
    pl.when(swapped)(lambda: greet(partner))
    pl.when(share > 0)(lambda: greet(worker(layer, share - 1)))
    scattered = (x == 0) & jnp.logical_not((d == 0) & (c == 0))
    pl.when(scattered)(lambda: greet((layer, 0)))

    gown[...] = jnp.broadcast_to(gain[...].astype(F32), (8, D))
    blocks = lax.broadcasted_iota(jnp.int32, (8, 512), 1) // 128 + 4 * d
    row = lax.broadcasted_iota(jnp.int32, (8, 512), 0)
    picked = [
        (blocks == rb[b, 0]) | (blocks == rb[b, 1]) | (blocks == rb[b, 2]) for b in range(2)
    ]
    zero, never = jnp.zeros((8, 512), F32), jnp.full((8, 512), -jnp.inf, F32)
    bown[...] = jnp.where(row == 0, jnp.where(picked[0], zero, never), jnp.where(picked[1], zero, never))

    extra = jnp.where(is_source, 15 + c, 0)
    pl.semaphore_wait(bar, 7 + swapped.astype(jnp.int32) + (share < 63).astype(jnp.int32) + extra)

    sends, tokens, seen = [], {}, set()

    def push(token, src, dev, recv=None, dst=None):
        i = len(tokens)
        tokens[token] = (src if recv is None else recv, i)
        copy = pltpu.make_async_remote_copy(
            src, src if dst is None else dst, all_s.at[i], all_r.at[i], device_id=dev, device_id_type=MESH
        )
        copy.start()
        sends.append(copy)

    def arrived(ref, sem):
        pltpu.make_async_copy(ref, ref, sem).wait()

    def await_token(*names):
        for name in names:
            if name not in seen:
                seen.add(name)
                ref, i = tokens[name]
                arrived(ref, all_r.at[i])

    def entries(slot):
        pairs = []
        for j in range(KVH):
            at = GROUP * j
            for src, first, last in (
                (kvw.at[0, :, HD * j : HD * j + HD], at, at + 128),
                (kvw.at[0, :, KVD + HD * j : KVD + HD * j + HD], at + 128, at + 256),
                (qw.at[0, :, 512 * j : 512 * j + 512], at + 256, at + 768),
            ):
                pairs.append((src, W.at[slot, x, z, :, first:last]))
        pairs += [(gown, gbuf), (act.at[0], res), (bown, bbuf)]
        for j in range(KVH):
            for h in range(2):
                first = KVD * h + HD * j
                pairs.append((cache.at[0, :, first : first + HD], cbuf.at[j, h]))
        return pairs

    def trade_copy(k):
        src, dst = entries(yl)[k]
        return pltpu.make_async_remote_copy(
            src, dst, in_s.at[k], in_r.at[k], device_id=partner, device_id_type=MESH
        )

    def bring(first, last):
        def own():
            for k in range(first, last):
                src, dst = entries(yl)[k]
                pltpu.make_async_copy(src, dst, in_r.at[k]).start()

        def trade():
            for k in range(first, last):
                trade_copy(k).start()

        pl.when(jnp.logical_not(swapped))(own)
        pl.when(swapped)(trade)

    def brought(*which):
        for k in which:
            if k not in seen:
                seen.add(k)
                arrived(entries(c)[k][1], in_r.at[k])

    def scatter_copy(ct, zt):
        return pltpu.make_async_remote_copy(
            cache.at[0, ROWS * zt : ROWS * zt + ROWS, 512 * ct : 512 * ct + 512], G.at[ct, zt],
            gs_s.at[8 * ct + zt], gs_r.at[0],
            device_id=(2 * yh + ct, 32 * c + zt), device_id_type=MESH,
        )

    def scatter(act_on):
        for ct in range(2):
            for zt in range(8):
                if (ct, zt) == (0, 0):
                    pl.when(c == 1)(lambda: act_on(scatter_copy(0, 0)))
                else:
                    act_on(scatter_copy(ct, zt))

    def spread_copy(k):
        return pltpu.make_async_remote_copy(
            G.at[c, z], G.at[c, z], gx_s.at[k - 1], gx_r.at[0], device_id=xdev(k), device_id_type=MESH
        )

    def spread(act_on):
        for k in range(1, NX):
            act_on(spread_copy(k))

    def halves(k, size):
        return (slice(0, size // 2), slice(size // 2, size)) if k == 3 else (slice(0, size),) * 2

    def ring(tag, k, block, size):
        a, b = halves(k, size)
        push((tag, "r", k + 1), block(zat(-k), a), zdev(1), block(zat(-k - 1), a))
        push((tag, "l", k + 1), block(zat(k), b), zdev(-1), block(zat(k + 1), b))

    def step_u(_, k):
        def block(at, part):
            return G.at[c, at, part]

        if k == 0:
            pl.when(x == 0)(lambda: arrived(G.at[c, z], gs_r.at[0]))
            pl.when(x == 0)(lambda: spread(lambda copy: copy.start()))
            return
        k -= 1
        if k == 0:
            pl.when(x != 0)(lambda: arrived(G.at[c, z], gx_r.at[0]))
        else:
            await_token(("U", "r", k), ("U", "l", k))
        if k < 4:
            ring("U", k, block, 32)
        else:
            push("Us", G.at[c], sibling, G.at[1 - c])

    def columns_a(p):
        return slice(GROUP * p, GROUP * p + SPLIT[p])

    def columns_b(p):
        return slice(GROUP * p + SPLIT[p], GROUP * (p + 1))

    def offsets(k):
        return (0,) if k == 0 else (4,) if k == 4 else (-k, k)

    def step_a(p, k):
        cols = columns_a(p)

        def block(at, part):
            return W.at[c, part, at, :, cols]

        if k == 0:
            brought(3 * p, 3 * p + 1, 3 * p + 2)
            for i in (1, -1, 2):
                push(("A", p, "x", i), W.at[c, x, z, :, cols], xdev(i), W.at[c, xat(-i), z, :, cols])
            return
        k -= 1
        if k == 0:
            await_token(*(("A", p, "x", i) for i in (1, -1, 2)))
        else:
            await_token((("A", p), "r", k), (("A", p), "l", k))
        if k < 4:
            ring(("A", p), k, block, 4)
        else:
            push(("A", p, "s"), W.at[c, :, :, :, cols], sibling, W.at[1 - c, :, :, :, cols])

    def hand_b(p, i, xo):
        cols = columns_b(p)
        push(("B", p, "s", i), W.at[c, xat(xo), :, :, cols], sibling, W.at[1 - c, xat(xo), :, :, cols])

    def step_b(p, k):
        cols = columns_b(p)

        def block(at, part):
            return W.at[c, x, at, part, cols]

        if k == 0:
            brought(3 * p, 3 * p + 1, 3 * p + 2)
        else:
            await_token((("B", p), "r", k), (("B", p), "l", k))
        if k < 4:
            ring(("B", p), k, block, 32)
        for q in offsets(k):
            mine = W.at[c, x, zat(q), :, cols]
            push(("B", p, "a", q), mine, xdev(1), W.at[c, xat(-1), zat(q), :, cols])
            push(("B", p, "b", q), mine, xdev(-1), W.at[c, xat(1), zat(q), :, cols])
        if k == 4:
            hand_b(p, 0, 0)

    def step_f(p, k):
        cols = columns_b(p)

        def along(xo, q, part):
            return W.at[c, xat(xo), zat(q), part, cols]

        await_token(*(("B", p, way, q) for way in "ab" for q in offsets(k)))
        if k in (0, 4):
            up, down, qa, qb_ = slice(0, 16), slice(16, 32), k, k
        else:
            up, down, qa, qb_ = slice(0, 32), slice(0, 32), -k, k
        push(("F", p, "a", k), along(-1, qa, up), xdev(1), along(2, qa, up))
        push(("F", p, "b", k), along(1, qb_, down), xdev(-1), along(2, qb_, down))

    def step_g(p, k):
        if k == 0:
            await_token(*(("B", p, way, q) for way in "ab" for q in range(-3, 5)))
            hand_b(p, 1, -1)
            hand_b(p, 2, 1)
        else:
            await_token(*(("F", p, way, q) for way in "ab" for q in range(5)))
            hand_b(p, 3, 2)

    def half_shared(p):
        if SPLIT[p]:
            await_token(("A", p, "s"))
        if SPLIT[p] < GROUP:
            await_token(*(("B", p, "s", i) for i in range(4)))

    def step_c(*_):
        bring(15, 23)

    def step_n(*_):
        brought(12, 13)

        @pl.loop(0, TOK // 32)
        def _(i):
            rows = pl.ds(pl.multiple_of(i * 32, 32), 32)
            wide = res[rows, :].astype(F32)
            spread_ = jnp.mean(wide * wide, axis=-1, keepdims=True)
            nb[rows, :] = (wide * lax.rsqrt(spread_ + EPS) * gbuf[0:1, :]).astype(BF16)

    halo_to = worker(layer, share + 1)

    def halo_copy(j):
        cols = slice(256 * j, 256 * j + 256)
        return pltpu.make_async_remote_copy(
            kv.at[256:384, cols], kv.at[0:128, cols], in_s.at[23 + j], in_r.at[23 + j],
            device_id=halo_to, device_id_type=MESH,
        )

    def step_q(j, _):
        half_shared(j)

        def times(first):
            w = W[:, :, :, :, GROUP * j + first : GROUP * j + first + 256].reshape(D, 256)
            return jnp.dot(nb[...], w, preferred_element_type=F32).astype(BF16)

        kv[128:384, 256 * j : 256 * j + 256] = times(0)
        pl.when(share < 63)(lambda: halo_copy(j).start())
        qb[j, :, 0:256] = times(256)
        qb[j, :, 256:512] = times(512)

    def step_t(j, b):
        brought(14, 15 + 2 * j, 16 + 2 * j)
        await_token("Us")
        if b == 0:
            pl.when(share > 0)(lambda: arrived(kv.at[0:128, 256 * j : 256 * j + 256], in_r.at[23 + j]))
        key = slice(HD * j, HD * j + HD)
        rows = slice(128 * b, 128 * b + 128)
        near = slice(128 * b, 128 * b + 256)
        near_key, near_value = slice(256 * j, 256 * j + 128), slice(256 * j + 128, 256 * j + 256)
        q4 = jnp.concatenate([qb[j, rows, HD * g : HD * g + HD] for g in range(4)], axis=0)

        def score(keys):
            return SCALE * lax.dot_general(q4, keys, (((1,), (1,)), ((), ())), preferred_element_type=F32)

        s_glob = score(G[0, :, :, key].reshape(256, HD))
        s_rand = score(cbuf[j, 0]) + bbuf[b : b + 1, :]
        at_row = lax.broadcasted_iota(jnp.int32, (512, 256), 0) % 128
        at_col = lax.broadcasted_iota(jnp.int32, (512, 256), 1)
        prior = at_col < 128
        if b == 0:
            prior = prior & (share > 0)
        own = (at_col >= 128) & (at_col - 128 <= at_row)
        s_near = jnp.where(prior | own, score(kv[near, near_key]), -jnp.inf)
        top = jnp.maximum(
            jnp.max(s_rand, axis=-1, keepdims=True),
            jnp.max(jnp.maximum(s_glob, s_near), axis=-1, keepdims=True),
        )
        e_glob, e_rand, e_near = jnp.exp2(s_glob - top), jnp.exp2(s_rand - top), jnp.exp2(s_near - top)
        total = jnp.sum(e_rand, axis=-1, keepdims=True) + jnp.sum(e_glob + e_near, axis=-1, keepdims=True)
        heads = jnp.dot(e_glob.astype(BF16), G[1, :, :, key].reshape(256, HD), preferred_element_type=F32)
        heads += jnp.dot(e_rand.astype(BF16), cbuf[j, 1], preferred_element_type=F32)
        heads += jnp.dot(e_near.astype(BF16), kv[near, near_value], preferred_element_type=F32)
        heads = heads / total
        for g in range(4):
            left = res[rows, 512 * j + HD * g : 512 * j + HD * g + HD].astype(F32)
            ob[j, rows, HD * g : HD * g + HD] = (left + heads[128 * g : 128 * g + 128]).astype(BF16)
        there = out.at[0, rows, 512 * j : 512 * j + 512]
        push(("o", j, b), ob.at[j, rows], target, there, there)

    pl.when(is_source)(lambda: scatter(lambda copy: copy.start()))
    pl.when(is_source & (c == 0))(
        lambda: pltpu.make_async_copy(cache.at[0, 0:ROWS, 0:512], G.at[0, 0], gs_r.at[0]).start()
    )
    bring(0, 15)

    def no_prior():
        kv[0:128, :] = jnp.zeros((128, 1024), BF16)

    pl.when(share == 0)(no_prior)
    steps = dict(
        A=step_a, B=step_b, F=step_f, G=step_g, U=step_u, c=step_c, n=step_n, q=step_q, t=step_t
    )
    for name, p, k in ORDER:
        steps[name](p, k)

    late = [i for i, token in enumerate(tokens) if token[0] == "o"]
    for i, copy in enumerate(sends):
        if i not in late:
            copy.wait_send()
    for j in range(KVH):
        pl.when(share < 63)(lambda j=j: halo_copy(j).wait_send())
    pl.when(is_source)(lambda: scatter(lambda copy: copy.wait_send()))
    pl.when(x == 0)(lambda: spread(lambda copy: copy.wait_send()))

    def traded():
        for k in range(23):
            trade_copy(k).wait_send()

    pl.when(swapped)(traded)
    await_token(*(("o", j, b) for j in range(KVH) for b in range(2)))
    for i in late:
        sends[i].wait_send()


def per_device(activations, norm_gain, query_weight, keyval_weight, prefix_cache, random_blocks):
    anywhere = pl.BlockSpec(memory_space=pl.ANY)
    dma = pltpu.SemaphoreType.DMA
    return pl.pallas_call(
        kernel,
        out_shape=pltpu.VMEM((1, TOK, D), BF16),
        in_specs=[
            anywhere, pl.BlockSpec(memory_space=pltpu.VMEM), anywhere, anywhere, anywhere,
            pl.BlockSpec(memory_space=pltpu.SMEM),
        ],
        out_specs=pl.BlockSpec(memory_space=pltpu.VMEM),
        scratch_shapes=[
            pltpu.VMEM((2, NX, NZ, ROWS, 3072), BF16),
            pltpu.VMEM((2, NZ, ROWS, 512), BF16),
            pltpu.VMEM((TOK, D), BF16),
            pltpu.VMEM((TOK, D), BF16),
            pltpu.VMEM((4, 2, 512, HD), BF16),
            pltpu.VMEM((384, 1024), BF16),
            pltpu.VMEM((4, TOK, 512), BF16),
            pltpu.VMEM((4, TOK, 512), BF16),
            pltpu.VMEM((8, D), F32),
            pltpu.VMEM((8, D), F32),
            pltpu.VMEM((8, 512), F32),
            pltpu.VMEM((8, 512), F32),
            dma((27,)), dma((27,)),
            dma((16,)), dma((1,)), dma((3,)), dma((1,)), dma((NTOKENS,)), dma((NTOKENS,)),
        ],
        compiler_params=pltpu.CompilerParams(
            collective_id=0, has_side_effects=True, vmem_limit_bytes=60 * 1024 * 1024
        ),
        cost_estimate=pl.CostEstimate(flops=5 * 10**9, bytes_accessed=2 * 10**7, transcendentals=4 * 10**6),
        name="relay_step",
    )(activations, norm_gain, query_weight, keyval_weight, prefix_cache, random_blocks)


def solution(mesh):
    return jax.shard_map(
        per_device,
        mesh=mesh,
        in_specs=(
            P("section", "dp", None),
            P("section", None),
            P("section", "dp", None),
            P("section", "dp", None),
            P("section", "dp", None),
            P("dp", None),
        ),
        out_specs=P("section", "dp", None),
        check_vma=False,
    )
```

```python
import math

import jax
import jax.numpy as jnp
from jax import lax
from jax.experimental import pallas as pl
from jax.experimental.pallas import tpu as pltpu
from jax.sharding import PartitionSpec as P

KVH = 4
HD = 128
D = 2048
KVD = 512
TOK = 256
NX, NZ = 4, 8
ROWS = 32
EPS = 1e-05
MESH = pl.DeviceIdType.MESH
F32, BF16 = jnp.float32, jnp.bfloat16
SCALE = math.log2(math.e) / math.sqrt(HD)

GROUP = 768
SPLIT = (256, 256, 256, 256)
NTOKENS = 217
ORDER = (
    ("A", 0, 0), ("B", 0, 0), ("A", 1, 0), ("B", 1, 0), ("U", 0, 0), ("B", 0, 1), ("c", 0, 0), ("A", 0, 1),
    ("F", 0, 0), ("B", 1, 1), ("A", 1, 1), ("F", 1, 0), ("B", 0, 2), ("U", 0, 1), ("A", 0, 2), ("B", 1, 2),
    ("F", 0, 1), ("A", 1, 2), ("F", 1, 1), ("B", 0, 3), ("A", 2, 0), ("B", 2, 0), ("U", 0, 2), ("F", 0, 2),
    ("n", 0, 0), ("A", 0, 3), ("B", 1, 3), ("F", 1, 2), ("A", 1, 3), ("B", 0, 4), ("A", 3, 0), ("F", 0, 3),
    ("B", 2, 1), ("U", 0, 3), ("B", 3, 0), ("A", 2, 1), ("F", 2, 0), ("A", 0, 4), ("B", 1, 4), ("F", 1, 3),
    ("A", 1, 4), ("B", 2, 2), ("F", 0, 4), ("G", 0, 0), ("U", 0, 4), ("B", 3, 1), ("A", 3, 1), ("A", 2, 2),
    ("A", 0, 5), ("F", 2, 1), ("A", 1, 5), ("F", 3, 0), ("B", 2, 3), ("U", 0, 5), ("F", 1, 4), ("G", 1, 0),
    ("B", 3, 2), ("A", 3, 2), ("F", 2, 2), ("G", 0, 1), ("A", 2, 3), ("B", 2, 4), ("F", 3, 1), ("B", 3, 3),
    ("q", 0, 0), ("G", 1, 1), ("F", 2, 3), ("A", 2, 4), ("A", 3, 3), ("F", 3, 2), ("B", 3, 4), ("t", 0, 1),
    ("q", 1, 0), ("A", 2, 5), ("F", 2, 4), ("G", 2, 0), ("F", 3, 3), ("A", 3, 4), ("F", 3, 4), ("G", 3, 0),
    ("t", 1, 1), ("G", 2, 1), ("t", 0, 0), ("A", 3, 5), ("G", 3, 1), ("q", 2, 0), ("t", 1, 0), ("q", 3, 0),
    ("t", 2, 1), ("t", 3, 1), ("t", 2, 0), ("t", 3, 0),
)


def kernel(
    act, gain, qw, kvw, cache, rb, out,
    W, G, res, nb, cbuf, kv, qb, ob, gown, gbuf, bown, bbuf,
    in_s, in_r, gs_s, gs_r, gx_s, gx_r, all_s, all_r,
):
    s, d = lax.axis_index("section"), lax.axis_index("dp")
    yh, c = lax.div(s, 2), lax.rem(s, 2)
    yl, xz = lax.div(d, 32), lax.rem(d, 32)
    x, z = lax.div(xz, NZ), lax.rem(xz, NZ)
    base = 32 * yl
    share, layer = 32 * c + xz, 2 * yh + yl
    swapped = c != yl

    def xat(k):
        return lax.rem(x + k + NX, NX)

    def zat(k):
        return lax.rem(z + k + NZ, NZ)

    def xdev(k):
        return (s, base + NZ * xat(k) + z)

    def zdev(k):
        return (s, base + NZ * x + zat(k))

    def worker(layer_, share_):
        return (2 * lax.div(layer_, 2) + lax.div(share_, 32), 32 * lax.rem(layer_, 2) + lax.rem(share_, 32))

    sibling = (2 * yh + 1 - c, d)
    partner = (2 * yh + 1 - c, 32 * (1 - yl) + xz)
    target = (lax.rem(layer + 1, 8), share)
    origin = worker(lax.rem(s + 7, 8), d)
    is_source = d == 0

    bar = pltpu.get_barrier_semaphore()

    def greet(dev):
        pl.semaphore_signal(bar, inc=1, device_id=dev, device_id_type=MESH)

    for dev in (xdev(1), xdev(-1), xdev(2), zdev(1), zdev(-1), sibling, origin):
        greet(dev)
    pl.when(swapped)(lambda: greet(partner))
    pl.when(share > 0)(lambda: greet(worker(layer, share - 1)))
    scattered = (x == 0) & jnp.logical_not((d == 0) & (c == 0))
    pl.when(scattered)(lambda: greet((layer, 0)))

    gown[...] = jnp.broadcast_to(gain[...].astype(F32), (8, D))
    blocks = lax.broadcasted_iota(jnp.int32, (8, 512), 1) // 128 + 4 * d
    row = lax.broadcasted_iota(jnp.int32, (8, 512), 0)
    picked = [
        (blocks == rb[b, 0]) | (blocks == rb[b, 1]) | (blocks == rb[b, 2]) for b in range(2)
    ]
    zero, never = jnp.zeros((8, 512), F32), jnp.full((8, 512), -jnp.inf, F32)
    bown[...] = jnp.where(row == 0, jnp.where(picked[0], zero, never), jnp.where(picked[1], zero, never))

    extra = jnp.where(is_source, 15 + c, 0)
    pl.semaphore_wait(bar, 7 + swapped.astype(jnp.int32) + (share < 63).astype(jnp.int32) + extra)

    sends, tokens, seen = [], {}, set()

    def push(token, src, dev, recv=None, dst=None):
        i = len(tokens)
        tokens[token] = (src if recv is None else recv, i)
        copy = pltpu.make_async_remote_copy(
            src, src if dst is None else dst, all_s.at[i], all_r.at[i], device_id=dev, device_id_type=MESH
        )
        copy.start()
        sends.append(copy)

    def arrived(ref, sem):
        pltpu.make_async_copy(ref, ref, sem).wait()

    def await_token(*names):
        for name in names:
            if name not in seen:
                seen.add(name)
                ref, i = tokens[name]
                arrived(ref, all_r.at[i])

    def entries(slot):
        pairs = []
        for j in range(KVH):
            at = GROUP * j
            for src, first, last in (
                (kvw.at[0, :, HD * j : HD * j + HD], at, at + 128),
                (kvw.at[0, :, KVD + HD * j : KVD + HD * j + HD], at + 128, at + 256),
                (qw.at[0, :, 512 * j : 512 * j + 512], at + 256, at + 768),
            ):
                pairs.append((src, W.at[slot, x, z, :, first:last]))
        pairs += [(gown, gbuf), (act.at[0], res), (bown, bbuf)]
        for j in range(KVH):
            for h in range(2):
                first = KVD * h + HD * j
                pairs.append((cache.at[0, :, first : first + HD], cbuf.at[j, h]))
        return pairs

    def trade_copy(k):
        src, dst = entries(yl)[k]
        return pltpu.make_async_remote_copy(
            src, dst, in_s.at[k], in_r.at[k], device_id=partner, device_id_type=MESH
        )

    def bring(first, last):
        def own():
            for k in range(first, last):
                src, dst = entries(yl)[k]
                pltpu.make_async_copy(src, dst, in_r.at[k]).start()

        def trade():
            for k in range(first, last):
                trade_copy(k).start()

        pl.when(jnp.logical_not(swapped))(own)
        pl.when(swapped)(trade)

    def brought(*which):
        for k in which:
            if k not in seen:
                seen.add(k)
                arrived(entries(c)[k][1], in_r.at[k])

    def scatter_copy(ct, zt):
        return pltpu.make_async_remote_copy(
            cache.at[0, ROWS * zt : ROWS * zt + ROWS, 512 * ct : 512 * ct + 512], G.at[ct, zt],
            gs_s.at[8 * ct + zt], gs_r.at[0],
            device_id=(2 * yh + ct, 32 * c + zt), device_id_type=MESH,
        )

    def scatter(act_on):
        for ct in range(2):
            for zt in range(8):
                if (ct, zt) == (0, 0):
                    pl.when(c == 1)(lambda: act_on(scatter_copy(0, 0)))
                else:
                    act_on(scatter_copy(ct, zt))

    def spread_copy(k):
        return pltpu.make_async_remote_copy(
            G.at[c, z], G.at[c, z], gx_s.at[k - 1], gx_r.at[0], device_id=xdev(k), device_id_type=MESH
        )

    def spread(act_on):
        for k in range(1, NX):
            act_on(spread_copy(k))

    def halves(k, size):
        return (slice(0, size // 2), slice(size // 2, size)) if k == 3 else (slice(0, size),) * 2

    def ring(tag, k, block, size):
        a, b = halves(k, size)
        push((tag, "r", k + 1), block(zat(-k), a), zdev(1), block(zat(-k - 1), a))
        push((tag, "l", k + 1), block(zat(k), b), zdev(-1), block(zat(k + 1), b))

    def step_u(_, k):
        def block(at, part):
            return G.at[c, at, part]

        if k == 0:
            pl.when(x == 0)(lambda: arrived(G.at[c, z], gs_r.at[0]))
            pl.when(x == 0)(lambda: spread(lambda copy: copy.start()))
            return
        k -= 1
        if k == 0:
            pl.when(x != 0)(lambda: arrived(G.at[c, z], gx_r.at[0]))
        else:
            await_token(("U", "r", k), ("U", "l", k))
        if k < 4:
            ring("U", k, block, 32)
        else:
            push("Us", G.at[c], sibling, G.at[1 - c])

    def columns_a(p):
        return slice(GROUP * p, GROUP * p + SPLIT[p])

    def columns_b(p):
        return slice(GROUP * p + SPLIT[p], GROUP * (p + 1))

    def offsets(k):
        return (0,) if k == 0 else (4,) if k == 4 else (-k, k)

    def step_a(p, k):
        cols = columns_a(p)

        def block(at, part):
            return W.at[c, part, at, :, cols]

        if k == 0:
            brought(3 * p, 3 * p + 1, 3 * p + 2)
            for i in (1, -1, 2):
                push(("A", p, "x", i), W.at[c, x, z, :, cols], xdev(i), W.at[c, xat(-i), z, :, cols])
            return
        k -= 1
        if k == 0:
            await_token(*(("A", p, "x", i) for i in (1, -1, 2)))
        else:
            await_token((("A", p), "r", k), (("A", p), "l", k))
        if k < 4:
            ring(("A", p), k, block, 4)
        else:
            push(("A", p, "s"), W.at[c, :, :, :, cols], sibling, W.at[1 - c, :, :, :, cols])

    def hand_b(p, i, xo):
        cols = columns_b(p)
        push(("B", p, "s", i), W.at[c, xat(xo), :, :, cols], sibling, W.at[1 - c, xat(xo), :, :, cols])

    def step_b(p, k):
        cols = columns_b(p)

        def block(at, part):
            return W.at[c, x, at, part, cols]

        if k == 0:
            brought(3 * p, 3 * p + 1, 3 * p + 2)
        else:
            await_token((("B", p), "r", k), (("B", p), "l", k))
        if k < 4:
            ring(("B", p), k, block, 32)
        for q in offsets(k):
            mine = W.at[c, x, zat(q), :, cols]
            push(("B", p, "a", q), mine, xdev(1), W.at[c, xat(-1), zat(q), :, cols])
            push(("B", p, "b", q), mine, xdev(-1), W.at[c, xat(1), zat(q), :, cols])
        if k == 4:
            hand_b(p, 0, 0)

    def step_f(p, k):
        cols = columns_b(p)

        def along(xo, q, part):
            return W.at[c, xat(xo), zat(q), part, cols]

        await_token(*(("B", p, way, q) for way in "ab" for q in offsets(k)))
        if k in (0, 4):
            up, down, qa, qb_ = slice(0, 16), slice(16, 32), k, k
        else:
            up, down, qa, qb_ = slice(0, 32), slice(0, 32), -k, k
        push(("F", p, "a", k), along(-1, qa, up), xdev(1), along(2, qa, up))
        push(("F", p, "b", k), along(1, qb_, down), xdev(-1), along(2, qb_, down))

    def step_g(p, k):
        if k == 0:
            await_token(*(("B", p, way, q) for way in "ab" for q in range(-3, 5)))
            hand_b(p, 1, -1)
            hand_b(p, 2, 1)
        else:
            await_token(*(("F", p, way, q) for way in "ab" for q in range(5)))
            hand_b(p, 3, 2)

    def half_shared(p):
        if SPLIT[p]:
            await_token(("A", p, "s"))
        if SPLIT[p] < GROUP:
            await_token(*(("B", p, "s", i) for i in range(4)))

    def step_c(*_):
        bring(15, 23)

    def step_n(*_):
        brought(12, 13)

        @pl.loop(0, TOK // 32)
        def _(i):
            rows = pl.ds(pl.multiple_of(i * 32, 32), 32)
            wide = res[rows, :].astype(F32)
            spread_ = jnp.mean(wide * wide, axis=-1, keepdims=True)
            nb[rows, :] = (wide * lax.rsqrt(spread_ + EPS) * gbuf[0:1, :]).astype(BF16)

    halo_to = worker(layer, share + 1)

    def halo_copy(j):
        cols = slice(256 * j, 256 * j + 256)
        return pltpu.make_async_remote_copy(
            kv.at[256:384, cols], kv.at[0:128, cols], in_s.at[23 + j], in_r.at[23 + j],
            device_id=halo_to, device_id_type=MESH,
        )

    def step_q(j, _):
        half_shared(j)

        def times(first):
            w = W[:, :, :, :, GROUP * j + first : GROUP * j + first + 256].reshape(D, 256)
            return jnp.dot(nb[...], w, preferred_element_type=F32).astype(BF16)

        kv[128:384, 256 * j : 256 * j + 256] = times(0)
        pl.when(share < 63)(lambda: halo_copy(j).start())
        qb[j, :, 0:256] = times(256)
        qb[j, :, 256:512] = times(512)

    def step_t(j, b):
        brought(14, 15 + 2 * j, 16 + 2 * j)
        await_token("Us")
        if b == 0:
            pl.when(share > 0)(lambda: arrived(kv.at[0:128, 256 * j : 256 * j + 256], in_r.at[23 + j]))
        key = slice(HD * j, HD * j + HD)
        rows = slice(128 * b, 128 * b + 128)
        near = slice(128 * b, 128 * b + 256)
        near_key, near_value = slice(256 * j, 256 * j + 128), slice(256 * j + 128, 256 * j + 256)
        q4 = jnp.concatenate([qb[j, rows, HD * g : HD * g + HD] for g in range(4)], axis=0)

        def score(keys):
            return SCALE * lax.dot_general(q4, keys, (((1,), (1,)), ((), ())), preferred_element_type=F32)

        s_glob = score(G[0, :, :, key].reshape(256, HD))
        s_rand = score(cbuf[j, 0]) + bbuf[b : b + 1, :]
        at_row = lax.broadcasted_iota(jnp.int32, (512, 256), 0) % 128
        at_col = lax.broadcasted_iota(jnp.int32, (512, 256), 1)
        prior = at_col < 128
        if b == 0:
            prior = prior & (share > 0)
        own = (at_col >= 128) & (at_col - 128 <= at_row)
        s_near = jnp.where(prior | own, score(kv[near, near_key]), -jnp.inf)
        top = jnp.maximum(
            jnp.max(s_rand, axis=-1, keepdims=True),
            jnp.max(jnp.maximum(s_glob, s_near), axis=-1, keepdims=True),
        )
        e_glob, e_rand, e_near = jnp.exp2(s_glob - top), jnp.exp2(s_rand - top), jnp.exp2(s_near - top)
        total = jnp.sum(e_rand, axis=-1, keepdims=True) + jnp.sum(e_glob + e_near, axis=-1, keepdims=True)
        heads = jnp.dot(e_glob.astype(BF16), G[1, :, :, key].reshape(256, HD), preferred_element_type=F32)
        heads += jnp.dot(e_rand.astype(BF16), cbuf[j, 1], preferred_element_type=F32)
        heads += jnp.dot(e_near.astype(BF16), kv[near, near_value], preferred_element_type=F32)
        heads = heads / total
        for g in range(4):
            left = res[rows, 512 * j + HD * g : 512 * j + HD * g + HD].astype(F32)
            ob[j, rows, HD * g : HD * g + HD] = (left + heads[128 * g : 128 * g + 128]).astype(BF16)
        there = out.at[0, rows, 512 * j : 512 * j + 512]
        push(("o", j, b), ob.at[j, rows], target, there, there)

    pl.when(is_source)(lambda: scatter(lambda copy: copy.start()))
    pl.when(is_source & (c == 0))(
        lambda: pltpu.make_async_copy(cache.at[0, 0:ROWS, 0:512], G.at[0, 0], gs_r.at[0]).start()
    )
    bring(0, 15)

    def no_prior():
        kv[0:128, :] = jnp.zeros((128, 1024), BF16)

    pl.when(share == 0)(no_prior)
    steps = dict(
        A=step_a, B=step_b, F=step_f, G=step_g, U=step_u, c=step_c, n=step_n, q=step_q, t=step_t
    )
    for name, p, k in ORDER:
        steps[name](p, k)

    late = [i for i, token in enumerate(tokens) if token[0] == "o"]
    for i, copy in enumerate(sends):
        if i not in late:
            copy.wait_send()
    for j in range(KVH):
        pl.when(share < 63)(lambda j=j: halo_copy(j).wait_send())
    pl.when(is_source)(lambda: scatter(lambda copy: copy.wait_send()))
    pl.when(x == 0)(lambda: spread(lambda copy: copy.wait_send()))

    def traded():
        for k in range(23):
            trade_copy(k).wait_send()

    pl.when(swapped)(traded)
    await_token(*(("o", j, b) for j in range(KVH) for b in range(2)))
    for i in late:
        sends[i].wait_send()


def per_device(activations, norm_gain, query_weight, keyval_weight, prefix_cache, random_blocks):
    anywhere = pl.BlockSpec(memory_space=pl.ANY)
    dma = pltpu.SemaphoreType.DMA
    return pl.pallas_call(
        kernel,
        out_shape=pltpu.VMEM((1, TOK, D), BF16),
        in_specs=[
            anywhere, pl.BlockSpec(memory_space=pltpu.VMEM), anywhere, anywhere, anywhere,
            pl.BlockSpec(memory_space=pltpu.SMEM),
        ],
        out_specs=pl.BlockSpec(memory_space=pltpu.VMEM),
        scratch_shapes=[
            pltpu.VMEM((2, NX, NZ, ROWS, 3072), BF16),
            pltpu.VMEM((2, NZ, ROWS, 512), BF16),
            pltpu.VMEM((TOK, D), BF16),
            pltpu.VMEM((TOK, D), BF16),
            pltpu.VMEM((4, 2, 512, HD), BF16),
            pltpu.VMEM((384, 1024), BF16),
            pltpu.VMEM((4, TOK, 512), BF16),
            pltpu.VMEM((4, TOK, 512), BF16),
            pltpu.VMEM((8, D), F32),
            pltpu.VMEM((8, D), F32),
            pltpu.VMEM((8, 512), F32),
            pltpu.VMEM((8, 512), F32),
            dma((27,)), dma((27,)),
            dma((16,)), dma((1,)), dma((3,)), dma((1,)), dma((NTOKENS,)), dma((NTOKENS,)),
        ],
        compiler_params=pltpu.CompilerParams(
            collective_id=0, has_side_effects=True, vmem_limit_bytes=60 * 1024 * 1024
        ),
        cost_estimate=pl.CostEstimate(flops=5 * 10**9, bytes_accessed=2 * 10**7, transcendentals=4 * 10**6),
        name="relay_step",
    )(activations, norm_gain, query_weight, keyval_weight, prefix_cache, random_blocks)


def solution(mesh):
    return jax.shard_map(
        per_device,
        mesh=mesh,
        in_specs=(
            P("section", "dp", None),
            P("section", None),
            P("section", "dp", None),
            P("section", "dp", None),
            P("section", "dp", None),
            P("dp", None),
        ),
        out_specs=P("section", "dp", None),
        check_vma=False,
    )
```
